128 devices in a mesh: replica: 8 (over x, core), expert: 16 (over z, y).
Axes of the slice: x: 4, y: 4, z: 4, core: 2. Of those that a mesh axis runs over, the one named last changes fastest.
Arguments:
- tokens: bfloat16 [1024, 3584], P(('replica', 'expert')), may hold values from -6 to 6
- queries: bfloat16 [1024, 36864], P(('replica', 'expert')), may hold values from -360 to 360
- latent_cache: bfloat16 [1024, 128, 576], P(('replica', 'expert')), may hold values from -6 to 6
- new_latent: bfloat16 [1024, 576], P(('replica', 'expert')), may hold values from -6 to 6
- lengths: int32 [1024], P(('replica', 'expert')), may hold values from 1 to 128
- finished: int32 [1024], P(('replica', 'expert')), may hold values 0 or 1
- migrate: int32 [128, 8, 1], P(('replica', 'expert')), may hold values from -1 to 7, as said below
- routes: int32 [2048, 8], P(('replica', 'expert')), may hold values from 0 to 127, all different within a row; in each aligned block of 16 rows (0 to 15, 16 to 31, ...) at most 2 rows name the same one
- route_score: float32 [2048, 8], P(('replica', 'expert')), may hold values from 0.05 to 1
- w_gate: bfloat16 [128, 3584, 1024], P(('replica', 'expert')), may hold values from -0.09375 to 0.09375
- w_up: bfloat16 [128, 3584, 1024], P(('replica', 'expert')), may hold values from -0.09375 to 0.09375
- w_down: bfloat16 [128, 1024, 3584], P(('replica', 'expert')), may hold values from -0.1875 to 0.1875
Outputs:
- attended: bfloat16 [2048, 32768], P(('replica', 'expert'))
- expert_out: bfloat16 [2048, 3584], P(('replica', 'expert'))
The draws below stay inside these ranges and needn't reach their ends.
Inputs may be any that keep to these rules, and one draw needn't show every extreme that they name: migrate[v, d, m] is a row of device v sent to the device of replica d with v's expert index, or -1 for none; a device names none of its rows twice and sends nothing to its own replica. `routes`: among the 16 work slots of one device no expert is named more than 2 times.
All inputs are finite; a program needn't handle non-finite values. No bound on the sum of `finished` on one device may be relied on, other than what follows from the above.
Results may differ from the reference program's by a relative error of at most 0.007.
Values may be sent and summed in bfloat16 or wider, within the bound.
No kernel may reach another device: no remote copies, remote signals or barrier semaphores. Data moves between devices by JAX's collectives and lax.ppermute only.
A program may use at most 128 MiB of HBM per device.

```python
import math
import jax
import jax.numpy as jnp
import numpy as np
from jax import lax

D = 3584
FF = 1024
HEADS = 64
VDIM = 512
TOPK = 8
MIG = 1
R_DEV = 8
CTX = 128
LAT = 576
EXPERTS = 128
ROWS = 1024
WORK = 16
WORKS = 2048
CAP = 2
N_REPLICA = 8
N_EXPERT = 16


def busy_replicas(key):
    ordering = jax.random.permutation(jax.random.fold_in(key, 101), N_REPLICA)
    return ordering < N_REPLICA // 2


def shuffle_rows(single_key):
    return jax.random.permutation(single_key, R_DEV)


def draw_latent_cache(key, part):
    key = jax.random.fold_in(key, 1)
    base = jnp.clip(jax.random.normal(key, (ROWS, CTX, LAT), jnp.float32), -6.0, 6.0)
    return base.astype(jnp.bfloat16)


def draw_queries(key, part):
    key = jax.random.fold_in(key, 2)
    base = jnp.clip(jax.random.normal(key, (ROWS, HEADS, LAT), jnp.float32), -6.0, 6.0)
    return base.reshape(ROWS, HEADS * LAT).astype(jnp.bfloat16)


def draw_new_latent(key, part):
    key = jax.random.fold_in(key, 3)
    base = jnp.clip(jax.random.normal(key, (ROWS, LAT), jnp.float32), -6.0, 6.0)
    return base.astype(jnp.bfloat16)


def draw_lengths(key, part):
    busy = busy_replicas(key)
    key = jax.random.fold_in(key, 4)
    row_busy = jnp.repeat(busy, N_EXPERT * R_DEV)
    long_length = jax.random.randint(jax.random.fold_in(key, 1), (ROWS,), CTX // 2, CTX + 1)
    short_length = jax.random.randint(jax.random.fold_in(key, 2), (ROWS,), 1, CTX // 4 + 1)
    result_length = jnp.where(row_busy, long_length, short_length)
    first_slot = jnp.arange(ROWS) % R_DEV == 0
    result_length = jnp.where(first_slot, jnp.where(row_busy, CTX, 1), result_length)
    return result_length.astype(jnp.int32)


def draw_migrate(key, part):
    busy = busy_replicas(key)
    key = jax.random.fold_in(key, 5)
    spare = jnp.logical_not(busy)
    spare_rank = jnp.cumsum(spare.astype(jnp.int32)) - 1
    device_keys = jax.random.split(key, N_REPLICA * N_EXPERT)
    orderings = jax.vmap(shuffle_rows)(device_keys)
    source_busy = jnp.repeat(busy, N_EXPERT)
    pick_index = spare_rank[:, None] * MIG + jnp.arange(MIG)[None, :]
    pick_index = jnp.clip(pick_index, 0, R_DEV - 1)
    slots_taken = orderings[:, pick_index]
    valid = source_busy[:, None, None] & spare[None, :, None]
    return jnp.where(valid, slots_taken, -1).astype(jnp.int32)


def with_ends(entries, stream_key, smallest, high):
    longest = entries.shape.index(max(entries.shape))
    spots = []
    for shift in (0, 1):
        where = [jax.random.randint(jax.random.fold_in(stream_key, axis), (), 0, length) for axis, length in enumerate(entries.shape)]
        where[longest] = (where[longest] + shift) % entries.shape[longest]
        spots.append(tuple(where))
    return entries.at[spots[0]].set(smallest).at[spots[1]].set(high)


def block_scale(key, shape, cuts, least, top_value):
    def one(dim, blocks):
        draws = jax.random.uniform(jax.random.fold_in(jax.random.fold_in(key, 6), dim), (blocks,), jnp.float32, least / len(cuts), top_value / len(cuts))
        return jnp.repeat(jnp.exp(draws), shape[dim] // blocks).reshape((-1,) + (1,) * (len(shape) - dim - 1))

    factor_of = one(*cuts[0])
    for cut in cuts[1:]:
        factor_of = factor_of * one(*cut)
    return factor_of


def assign_block(key, own, number, rows, count, top, bound, slope):
    ranking = jax.random.permutation(key, count)
    crowded, common = load_shares(count, rows * top, bound, slope, True), load_shares(count, rows * top, bound, slope, False)
    places = jnp.arange(count)

    def named(sizes, offset_by):
        used = int((sizes > 0).sum())
        fixed = max(1, used // 4)
        moved = fixed + (places - fixed + offset_by * (used - fixed)) % max(1, count - fixed)
        return jnp.zeros((count,), jnp.int32).at[ranking[jnp.where(places < fixed, places, moved)]].set(jnp.asarray(sizes, jnp.int32))

    sizes = jnp.where(number % 4 == 0, named(crowded, number // 4), named(common, number - number // 4 - 1))
    mixed = jax.random.permutation(jax.random.fold_in(own, 3), count)
    donor, sink = mixed[0:count // 2 * 2:2], mixed[1:count // 2 * 2:2]
    margin = jnp.minimum(sizes[donor] - 1, bound - sizes[sink]) // 2
    margin = jnp.where((donor == ranking[0]) | (sink == ranking[0]) | (sizes[sink] == 0), 0, jnp.maximum(margin, 0))
    moved = jax.random.randint(jax.random.fold_in(own, 4), (count // 2,), 0, 1 << 20) % (margin + 1)
    sizes = sizes.at[donor].add(-moved).at[sink].add(moved)
    labels = jnp.searchsorted(jnp.cumsum(sizes), jnp.arange(rows * top), side="right").astype(jnp.int32)
    grid = labels.reshape(top, rows).T
    grid = grid[jax.random.permutation(jax.random.fold_in(own, 1), rows)]
    offset_by = jax.random.randint(jax.random.fold_in(own, 2), (rows, 1), 0, top)
    return jnp.take_along_axis(grid, (jnp.arange(top)[None, :] + offset_by) % top, axis=1)


def load_shares(count, total, bound, skew, full):
    loads = [(1 << 20) // math.isqrt(standing ** skew) + 1 for standing in range(1, count + 1)]
    largest = bound if full else min(bound, max(-(-total // count), total * loads[0] // sum(loads)))
    least = 1 if total - largest >= count - 1 else 0
    given, surplus = [largest] + [least] * (count - 1), total - largest - least * (count - 1)
    while surplus > 0:
        movable = [i for i in range(1, count) if given[i] < largest] or [i for i in range(1, count) if given[i] < bound]
        pool, left = sum([loads[i] for i in movable]), surplus
        for i in movable:
            more = min(bound - given[i], max(1, left * loads[i] // pool), surplus)
            given[i] = given[i] + more
            surplus = surplus - more
    return np.array(given)


def centred(stream_key, dims, spread, bound, shards=(), kind=jnp.bfloat16):
    values = spread * jax.random.normal(stream_key, dims, jnp.float32)
    if shards:
        values = values * block_scale(stream_key, dims, shards, -0.22, 0.18)
    return jnp.clip(values, -bound, bound).astype(kind)


def setup_inputs(seed: int = 0) -> dict:
    seeds = jax.random.split(jax.random.key(seed), 13)
    tokens = centred(seeds[0], (ROWS, D), 1.0, 6.0, ((0, 128),))
    queries = draw_queries(jax.random.fold_in(seeds[12], 71), 0)
    latent_cache = draw_latent_cache(jax.random.fold_in(seeds[12], 71), 0)
    new_latent = draw_new_latent(jax.random.fold_in(seeds[12], 71), 0)
    lengths = draw_lengths(jax.random.fold_in(seeds[12], 71), 0)
    finished = with_ends((jax.random.randint(seeds[5], (ROWS,), 0, 16) < 1).astype(jnp.int32), jax.random.fold_in(seeds[5], 1), 0, 1)
    migrate = draw_migrate(jax.random.fold_in(seeds[12], 71), 0)
    routes_keys = jax.random.split(jax.random.fold_in(seeds[7], 1), WORKS // WORK)
    routes_turns = jax.random.permutation(jax.random.fold_in(seeds[7], 3), WORKS // WORK)
    routes = jax.vmap(lambda own, number: assign_block(jax.random.fold_in(seeds[7], 2), own, number, WORK, EXPERTS, TOPK, CAP, 2))(routes_keys, routes_turns).reshape((WORKS, TOPK))
    route_score = jnp.clip(jnp.exp(math.log(1.0) - 2.9957323 * jax.random.uniform(seeds[8], (WORKS, TOPK), jnp.float32) ** block_scale(seeds[8], (WORKS, TOPK), ((0, 128),), -0.2, 0.2)), 0.05, 1.0)
    w_gate = centred(seeds[9], (EXPERTS, D, FF), D ** -0.5, 0.09375, ((0, 128),))
    w_up = centred(seeds[10], (EXPERTS, D, FF), D ** -0.5, 0.09375, ((0, 128),))
    w_down = centred(seeds[11], (EXPERTS, FF, D), FF ** -0.5, 0.1875, ((0, 128),))
    return dict(tokens=tokens, queries=queries, latent_cache=latent_cache, new_latent=new_latent, lengths=lengths, finished=finished, migrate=migrate, routes=routes, route_score=route_score, w_gate=w_gate, w_up=w_up, w_down=w_down)


score_scale = 192.0 ** -0.5


def attend(query_rows, latent_rows, own_latent, live_length):
    row_count = query_rows.shape[0]
    per_head = query_rows.reshape(row_count, HEADS, LAT).astype(jnp.float32)
    key_values = latent_rows.astype(jnp.float32)
    own_key = own_latent.astype(jnp.float32)
    scores = jnp.einsum("nhl,ntl->nht", per_head, key_values) * score_scale
    own_score = jnp.einsum("nhl,nl->nh", per_head, own_key) * score_scale
    visible = jnp.arange(latent_rows.shape[1])[None, None, :] < live_length[:, None, None]
    scores = jnp.where(visible, scores, -jnp.inf)
    largest = jnp.maximum(jnp.max(scores, axis=2), own_score)
    weights = jnp.exp(scores - largest[:, :, None])
    own_weight = jnp.exp(own_score - largest)
    denominator = jnp.sum(weights, axis=2) + own_weight
    rounded = lax.optimization_barrier(weights.astype(jnp.bfloat16)).astype(jnp.float32)
    own_rounded = lax.optimization_barrier(own_weight.astype(jnp.bfloat16)).astype(jnp.float32)
    context = jnp.einsum("nht,ntv->nhv", rounded, key_values[:, :, :VDIM])
    context = context + own_rounded[:, :, None] * own_key[:, None, :VDIM]
    normalized = context / denominator[:, :, None] * (live_length > 0).astype(jnp.float32)[:, None, None]
    return normalized.reshape(row_count, HEADS * VDIM).astype(jnp.bfloat16)


def reference(tokens, queries, latent_cache, new_latent, lengths, finished, migrate, routes, route_score, w_gate, w_up, w_down):
    device_count = N_REPLICA * N_EXPERT
    layout_plan = migrate.reshape(N_REPLICA, N_EXPERT, N_REPLICA, MIG)
    incoming = jnp.transpose(layout_plan, (2, 1, 0, 3))
    sender = jnp.arange(N_REPLICA)[None, None, :, None] * N_EXPERT + jnp.arange(N_EXPERT)[None, :, None, None]
    incoming_row = (sender * R_DEV + jnp.maximum(incoming, 0)).reshape(device_count, N_REPLICA * MIG)
    incoming_used = (incoming >= 0).reshape(device_count, N_REPLICA * MIG)
    leaving = jnp.arange(device_count)[:, None, None] * R_DEV + jnp.maximum(migrate, 0)
    leaving = jnp.where(migrate >= 0, leaving, ROWS)
    moved_flag = jnp.zeros((ROWS + 1,), jnp.int32).at[leaving.reshape(-1)].set(1)[:ROWS]
    local_row = jnp.arange(ROWS).reshape(device_count, R_DEV)
    local_used = moved_flag.reshape(device_count, R_DEV) == 0
    source = jnp.concatenate([local_row, incoming_row], axis=1).astype(jnp.int32)
    occupied = jnp.concatenate([local_used, incoming_used], axis=1)
    living = occupied & (finished[source] == 0)
    live_length = jnp.where(living, lengths[source], 0).astype(jnp.int32)

    def per_device(packed):
        row_index, length_row = packed
        return attend(queries[row_index], latent_cache[row_index], new_latent[row_index], length_row)

    attended = lax.map(per_device, (source, live_length)).reshape(WORKS, HEADS * VDIM)

    flat_living = living.reshape(-1)
    expert_input = jnp.where(flat_living[:, None], tokens[source.reshape(-1)], jnp.zeros_like(tokens[:1]))
    combine = 2.5 * route_score / jnp.sum(route_score, axis=1, keepdims=True)
    combine = combine * flat_living[:, None].astype(jnp.float32)
    chosen_expert = routes.reshape(device_count, WORK * TOPK)
    pair_alive = jnp.repeat(living, TOPK, axis=1)
    matches = ((chosen_expert[:, :, None] == jnp.arange(EXPERTS)[None, None, :]) & pair_alive[:, :, None]).astype(jnp.int32)
    position = jnp.sum((jnp.cumsum(matches, axis=1) - 1) * matches, axis=2)
    slot_index = (chosen_expert * device_count + jnp.arange(device_count)[:, None]) * CAP + position
    table_size = EXPERTS * device_count * CAP
    target = jnp.where(pair_alive, slot_index, table_size)
    pair_row = (jnp.arange(device_count)[:, None] * WORK + jnp.arange(WORK * TOPK)[None, :] // TOPK).astype(jnp.int32)
    slot_table = jnp.full((table_size + 1,), -1, jnp.int32).at[target.reshape(-1)].set(pair_row.reshape(-1))[:table_size]
    slot_table = slot_table.reshape(EXPERTS, device_count * CAP)

    def per_expert(packed):
        row_index, gate_matrix, up_matrix, down_matrix = packed
        selected = jnp.where((row_index >= 0)[:, None], expert_input[jnp.maximum(row_index, 0)], jnp.zeros_like(expert_input[:1]))
        gate_value = jnp.dot(selected, gate_matrix, preferred_element_type=jnp.float32)
        up_value = jnp.dot(selected, up_matrix, preferred_element_type=jnp.float32)
        hidden = (jax.nn.silu(gate_value) * up_value).astype(jnp.bfloat16)
        return jnp.dot(hidden, down_matrix, preferred_element_type=jnp.float32).astype(jnp.bfloat16)

    results = lax.map(per_expert, (slot_table, w_gate, w_up, w_down)).reshape(table_size, D)
    picked = results[jnp.clip(slot_index, 0, table_size - 1).reshape(-1)].astype(jnp.float32).reshape(WORKS, TOPK, D)
    expert_out = jnp.sum(picked * combine[:, :, None], axis=1).astype(jnp.bfloat16)
    return attended, expert_out
```

```python
import jax
import jax.numpy as jnp
from jax import lax
from jax.experimental import pallas as pl
from jax.experimental.pallas import tpu as pltpu
from jax.sharding import PartitionSpec as P

HEADS = 64
VDIM = 512
LAT = 576
BOTH = ("replica", "expert")
F32 = jnp.float32
BF16 = jnp.bfloat16

PARTS = 4
CAP = 2

DEVICE_ORDER = (
    23, 44, 105, 64, 100, 28, 5, 34, 111, 118, 84, 50, 77, 79, 37, 43,
    15, 120, 74, 83, 125, 69, 8, 19, 41, 88, 47, 102, 115, 17, 101, 127,
    55, 81, 78, 122, 13, 57, 65, 0, 126, 117, 40, 112, 1, 61, 66, 22,
    107, 76, 62, 89, 116, 103, 110, 36, 82, 30, 85, 9, 3, 95, 6, 51,
    16, 124, 75, 104, 121, 45, 38, 114, 26, 99, 72, 27, 42, 53, 97, 60,
    54, 87, 94, 73, 113, 7, 31, 52, 59, 29, 90, 4, 98, 49, 92, 11,
    21, 39, 48, 93, 10, 67, 123, 24, 32, 108, 63, 119, 12, 71, 14, 20,
    80, 33, 70, 58, 109, 68, 25, 86, 35, 96, 91, 56, 18, 106, 2, 46,
)

score_scale = 192.0 ** (-0.5)

VMEM = pl.BlockSpec(memory_space=pltpu.VMEM)
SMEM = pl.BlockSpec(memory_space=pltpu.SMEM)
HBM = pl.BlockSpec(memory_space=pltpu.HBM)


def iota(shape, dim):
    return lax.broadcasted_iota(jnp.int32, shape, dim)


def attend(query_rows, latent_rows, own_latent, live_length):
    row_count = query_rows.shape[0]
    per_head = query_rows.reshape(row_count, HEADS, LAT)
    scores = (
        jnp.einsum("nhl,ntl->nht", per_head, latent_rows, preferred_element_type=F32) * score_scale
    )
    own_score = jnp.einsum("nhl,nl->nh", per_head, own_latent, preferred_element_type=F32)
    own_score = own_score * score_scale
    visible = iota((1, 1, latent_rows.shape[1]), 2) < live_length[:, None, None]
    scores = jnp.where(visible, scores, -jnp.inf)
    largest = jnp.maximum(jnp.max(scores, axis=2), own_score)
    weights = jnp.exp(scores - largest[:, :, None])
    own_weight = jnp.exp(own_score - largest)
    denominator = jnp.sum(weights, axis=2) + own_weight
    context = jnp.einsum(
        "nht,ntv->nhv",
        weights.astype(BF16),
        latent_rows[:, :, :VDIM],
        preferred_element_type=F32,
    )
    own_rounded = lax.optimization_barrier(own_weight.astype(BF16)).astype(F32)
    context = context + own_rounded[:, :, None] * own_latent[:, None, :VDIM].astype(F32)
    normalized = context / denominator[:, :, None] * (live_length > 0).astype(F32)[:, None, None]
    return normalized.astype(BF16)


def by_index(index, count, value_of):
    spread = jnp.zeros(index.shape, jnp.int32)
    for i in range(count):
        spread = jnp.where(index == i, value_of(i), spread)
    return spread


def alive_of(length, finished):
    return lambda s: jnp.where(finished[s] == 0, length[s], 0)


def start_all(copies):
    for copy in copies:
        copy.start()
    return copies


def wait_all(copies):
    for copy in copies:
        copy.wait()


def sub_rows(rows, width):
    pieces = [rows[:, q * width : (q + 1) * width].astype(F32) for q in range(PARTS)]
    return jnp.concatenate(pieces, axis=0).astype(BF16)


def pick_kernel(plan_hbm, length_hbm, finished_hbm, tokens_hbm, out, *scratch):
    plan, length, finished, tokens, send, sems = scratch
    pairs = [
        (plan_hbm, plan),
        (length_hbm, length),
        (finished_hbm, finished),
        (tokens_hbm, tokens),
    ]
    wait_all(start_all([pltpu.make_async_copy(*pair, sems.at[n]) for n, pair in enumerate(pairs)]))
    count = tokens.shape[0]
    shape = (send.shape[0], PARTS * count)
    row, col = iota(shape, 0), iota(shape, 1)
    source = col & (count - 1)
    wanted = by_index(row >> 3, send.shape[0] // 8, lambda d: plan[d])
    alive = by_index(source, count, alive_of(length, finished))
    chosen = (wanted == source) & ((row & 7) == (col >> 3)) & (alive > 0)
    chosen = jnp.where(chosen, 1.0, 0.0).astype(BF16)
    flat = sub_rows(tokens[...], send.shape[1])
    send[...] = jnp.dot(chosen, flat, preferred_element_type=F32).astype(BF16)
    wait_all(start_all([pltpu.make_async_copy(send, out, sems.at[0])]))


def routing_kernel(plan, length, finished, routes, score, order, scatter, gather):
    slots, top = routes.shape
    lanes = scatter.shape[0]
    experts = lanes // 8
    count = slots // 2
    names = routes[...]
    scores = score[...]
    named = jnp.zeros((slots, experts), F32)
    weight = jnp.zeros((slots, experts), F32)
    for k in range(top):
        hit = names[:, k : k + 1] == order[...]
        named = jnp.where(hit, 1.0, named)
        weight = jnp.where(hit, scores[:, k : k + 1], weight)
    weight = 2.5 * weight / jnp.sum(scores, axis=1, keepdims=True)
    lower = jnp.where(iota((slots, slots), 1) < iota((slots, slots), 0), 1.0, 0.0).astype(BF16)
    position = jnp.dot(lower, named.astype(BF16), preferred_element_type=F32)
    high = weight.astype(BF16).astype(F32)
    low = weight - high
    stacked = jnp.concatenate([named, position, high, low], axis=0).astype(BF16)
    widen = iota((experts, lanes), 0) == (iota((experts, lanes), 1) >> 3)
    wide = jnp.dot(stacked, jnp.where(widen, 1.0, 0.0).astype(BF16), preferred_element_type=F32)
    lane = iota((slots, lanes), 1)
    part = lane & (PARTS - 1)
    place = ((lane >> 2) & 1).astype(F32)
    taken = (wide[:slots] > 0.5) & (wide[slots : 2 * slots] == place)
    taken = jnp.where(taken, 1.0, 0.0)

    row = iota((count, lanes), 0)
    alive = by_index(row, count, alive_of(length, finished))
    moved = jnp.zeros((count, lanes), jnp.int32)
    for d in range(count):
        moved = jnp.where(row == plan[d], 1, moved)
    stays = (alive > 0) & (moved == 0)
    half = part[:count]
    pieces = [jnp.where(stays & (half == q), taken[:count], 0.0) for q in range(PARTS)]
    for i in range(count):
        pieces.append(jnp.where(half == row, taken[count + i : count + i + 1], 0.0))
    used = len(pieces) * count
    pieces.append(jnp.zeros((scatter.shape[1] - used, lanes), F32))
    scatter[...] = jnp.transpose(jnp.concatenate(pieces, axis=0)).astype(BF16)

    pieces = []
    for start in (2 * slots, 3 * slots):
        wanted = wide[start : start + slots] * taken
        pieces += [jnp.where(part == q, wanted, 0.0) for q in range(PARTS)]
    gather[...] = jnp.concatenate(pieces, axis=0).astype(BF16)


def dispatch_kernel(scatter, tokens, arrived, out, block, sems):
    lanes, width = out.shape
    pad = scatter.shape[1] - PARTS * tokens.shape[0] - arrived.shape[0]
    pieces = [tokens[:, q * width : (q + 1) * width].astype(F32) for q in range(PARTS)]
    pieces += [arrived[...].astype(F32), jnp.zeros((pad, width), F32)]
    flat = jnp.concatenate(pieces, axis=0).astype(BF16)
    copies = []
    for b in range(lanes // 256):
        part = pl.ds(b * 256, 256)
        rows = jnp.dot(scatter[part, :], flat, preferred_element_type=F32)
        block[part, :] = rows.astype(BF16)
        copies += start_all([pltpu.make_async_copy(block.at[part], out.at[part], sems.at[b])])
    wait_all(copies)


def expert_kernel(recv, w_gate, w_up, w_down, out, rows, hidden, results, sent, sems):
    width = recv.shape[1]
    blocks = recv.shape[0] // 256
    one, two = iota((256, 256), 0), iota((256, 256), 1)
    apart = ((one & 63) * PARTS + (one >> 6)) == two
    together = ((two & 63) * PARTS + (two >> 6)) == one
    apart = jnp.where(apart, 1.0, 0.0).astype(BF16)
    together = jnp.where(together, 1.0, 0.0).astype(BF16)
    for b in range(blocks):
        got = jnp.dot(apart, recv[b * 256 : (b + 1) * 256, :], preferred_element_type=F32)
        got = got.astype(BF16)
        for q in range(PARTS):
            rows[q, b * 64 : (b + 1) * 64, :] = got[q * 64 : (q + 1) * 64, :]

    gate = up = None
    for q in range(PARTS):
        part = slice(q * width, (q + 1) * width)
        more = jnp.dot(rows[q], w_gate[0, part, :], preferred_element_type=F32)
        gate = more if gate is None else gate + more
        more = jnp.dot(rows[q], w_up[0, part, :], preferred_element_type=F32)
        up = more if up is None else up + more
    hidden[...] = (gate / (1.0 + jnp.exp(-gate)) * up).astype(BF16)
    for q in range(PARTS):
        part = slice(q * width, (q + 1) * width)
        result = jnp.dot(hidden[...], w_down[0, :, part], preferred_element_type=F32).astype(BF16)
        for b in range(blocks):
            results[b, q * 64 : (q + 1) * 64, :] = result[b * 64 : (b + 1) * 64, :]
    copies = []
    for b in range(blocks):
        part = pl.ds(b * 256, 256)
        value = jnp.dot(together, results[b], preferred_element_type=F32).astype(BF16)
        sent[part, :] = value
        copies += start_all([pltpu.make_async_copy(sent.at[part], out.at[part], sems.at[b])])
    wait_all(copies)


def combine_kernel(gather, recv, out):
    slots = out.shape[0]
    width = recv.shape[1]
    summed = jnp.dot(gather[...], recv[...], preferred_element_type=F32)
    half = summed.shape[0] // 2
    summed = summed[:half] + summed[half:]
    for q in range(PARTS):
        out[:, q * width : (q + 1) * width] = summed[q * slots : (q + 1) * slots].astype(BF16)


def call(kernel, outs, in_specs, cost, scratch=(), limit=32, in_hbm=False):
    shape_of = pltpu.HBM if in_hbm else jax.ShapeDtypeStruct
    shapes = [shape_of(shape, BF16) for shape in outs]
    specs = [HBM if in_hbm else VMEM] * len(outs)
    return pl.pallas_call(
        kernel,
        out_shape=shapes if len(shapes) > 1 else shapes[0],
        in_specs=in_specs,
        out_specs=specs if len(specs) > 1 else specs[0],
        scratch_shapes=list(scratch),
        compiler_params=pltpu.CompilerParams(vmem_limit_bytes=limit * 2**20),
        cost_estimate=pl.CostEstimate(flops=cost[0], bytes_accessed=cost[1], transcendentals=0),
    )


def on_device(
    tokens,
    queries,
    latent_cache,
    new_latent,
    lengths,
    finished,
    migrate,
    routes,
    route_score,
    w_gate,
    w_up,
    w_down,
):
    count, model = tokens.shape
    slots = routes.shape[0]
    replicas = lax.axis_size("replica")
    devices = replicas * lax.axis_size("expert")
    width = model // PARTS
    lanes = devices * CAP * PARTS
    hidden = w_gate.shape[2]
    plan = migrate.reshape(replicas)

    order = [list(DEVICE_ORDER)] if devices == len(DEVICE_ORDER) else [list(range(devices))]
    spread = jnp.broadcast_to(jnp.asarray(order, jnp.int32), (slots, devices))

    def exchange(values):
        values = values.reshape(devices, 8, width)
        values = lax.all_to_all(values, BOTH, 0, 0, axis_index_groups=order, tiled=True)
        return values.reshape(lanes, width)

    send = call(
        pick_kernel,
        [(replicas * 8, width)],
        [HBM] * 4,
        (10**6, 10**5),
        [
            pltpu.SMEM((replicas,), jnp.int32),
            pltpu.SMEM((count,), jnp.int32),
            pltpu.SMEM((count,), jnp.int32),
            pltpu.VMEM((count, model), BF16),
            pltpu.VMEM((replicas * 8, width), BF16),
            pltpu.SemaphoreType.DMA((4,)),
        ],
        in_hbm=True,
    )(*[pltpu.with_memory_space_constraint(x, pltpu.HBM) for x in (plan, lengths, finished, tokens)])
    arrived = lax.all_to_all(
        send.reshape(replicas, 8, width), "replica", split_axis=0, concat_axis=0, tiled=True
    ).reshape(replicas * 8, width)
    scatter, gather = call(
        routing_kernel,
        [(lanes, 128), (2 * PARTS * slots, lanes)],
        [SMEM] * 3 + [VMEM] * 3,
        (10**7, 10**6),
    )(plan, lengths, finished, routes, route_score, spread)
    outgoing = call(
        dispatch_kernel,
        [(lanes, width)],
        [VMEM] * 3,
        (2 * 10**8, 2 * 10**6),
        [pltpu.VMEM((lanes, width), BF16), pltpu.SemaphoreType.DMA((lanes // 256,))],
        in_hbm=True,
    )(scatter, tokens, arrived)
    incoming = exchange(outgoing)

    own_length = jnp.where(finished == 0, lengths, 0)
    attended = attend(queries, latent_cache, new_latent, own_length)
    sending = plan >= 0
    moved_out = jnp.any((plan[:, None] == jnp.arange(count)[None, :]), axis=0)
    leave = jnp.where(sending[:, None, None], attended[jnp.maximum(plan, 0)], jnp.zeros((), BF16))
    leave, incoming = lax.optimization_barrier((leave, incoming))
    landed = lax.all_to_all(leave, "replica", split_axis=0, concat_axis=0, tiled=True)
    stay = jnp.where(moved_out[:, None, None], jnp.zeros((), BF16), attended)
    attended_out = jnp.concatenate([stay, landed], axis=0).reshape(slots, HEADS * VDIM)

    results = call(
        expert_kernel,
        [(lanes, width)],
        [VMEM] * 4,
        (6 * devices * CAP * model * hidden, 6 * 10**6),
        [
            pltpu.VMEM((PARTS, devices * CAP, width), BF16),
            pltpu.VMEM((devices * CAP, hidden), BF16),
            pltpu.VMEM((lanes // 256, 256, width), BF16),
            pltpu.VMEM((lanes, width), BF16),
            pltpu.SemaphoreType.DMA((lanes // 256,)),
        ],
        24,
        True,
    )(incoming, *[pltpu.with_memory_space_constraint(w, pltpu.VMEM) for w in (w_gate, w_up, w_down)])
    returned = exchange(results)
    expert_out = call(combine_kernel, [(slots, model)], [VMEM] * 2, (2 * 10**8, 2 * 10**6))(
        gather, returned
    )
    return (attended_out, expert_out)


def solution(mesh):
    rows = P(BOTH, None)
    blocks = P(BOTH, None, None)
    flat = P(BOTH)
    return jax.shard_map(
        on_device,
        mesh=mesh,
        in_specs=(rows, rows, blocks, rows, flat, flat, blocks, rows, rows, blocks, blocks, blocks),
        out_specs=(rows, rows),
        check_vma=False,
    )
```

```python
import jax
import jax.numpy as jnp
from jax import lax
from jax.experimental import pallas as pl
from jax.experimental.pallas import tpu as pltpu
from jax.sharding import PartitionSpec as P

HEADS = 64
VDIM = 512
LAT = 576
BOTH = ("replica", "expert")
F32 = jnp.float32
BF16 = jnp.bfloat16

PARTS = 4
CAP = 2

score_scale = 192.0 ** (-0.5)

VMEM = pl.BlockSpec(memory_space=pltpu.VMEM)
SMEM = pl.BlockSpec(memory_space=pltpu.SMEM)
HBM = pl.BlockSpec(memory_space=pltpu.HBM)


def iota(shape, dim):
    return lax.broadcasted_iota(jnp.int32, shape, dim)


def attend(query_rows, latent_rows, own_latent, live_length):
    row_count = query_rows.shape[0]
    per_head = query_rows.reshape(row_count, HEADS, LAT)
    scores = (
        jnp.einsum("nhl,ntl->nht", per_head, latent_rows, preferred_element_type=F32) * score_scale
    )
    own_score = jnp.einsum("nhl,nl->nh", per_head, own_latent, preferred_element_type=F32)
    own_score = own_score * score_scale
    visible = iota((1, 1, latent_rows.shape[1]), 2) < live_length[:, None, None]
    scores = jnp.where(visible, scores, -jnp.inf)
    largest = jnp.maximum(jnp.max(scores, axis=2), own_score)
    weights = jnp.exp(scores - largest[:, :, None])
    own_weight = jnp.exp(own_score - largest)
    denominator = jnp.sum(weights, axis=2) + own_weight
    context = jnp.einsum(
        "nht,ntv->nhv",
        weights.astype(BF16),
        latent_rows[:, :, :VDIM],
        preferred_element_type=F32,
    )
    own_rounded = lax.optimization_barrier(own_weight.astype(BF16)).astype(F32)
    context = context + own_rounded[:, :, None] * own_latent[:, None, :VDIM].astype(F32)
    normalized = context / denominator[:, :, None] * (live_length > 0).astype(F32)[:, None, None]
    return normalized.astype(BF16)


def by_index(index, count, value_of):
    spread = jnp.zeros(index.shape, jnp.int32)
    for i in range(count):
        spread = jnp.where(index == i, value_of(i), spread)
    return spread


def alive_of(length, finished):
    return lambda s: jnp.where(finished[s] == 0, length[s], 0)


def start_all(copies):
    for copy in copies:
        copy.start()
    return copies


def wait_all(copies):
    for copy in copies:
        copy.wait()


def sub_rows(rows, width):
    pieces = [rows[:, q * width : (q + 1) * width].astype(F32) for q in range(PARTS)]
    return jnp.concatenate(pieces, axis=0).astype(BF16)


def pick_kernel(plan_hbm, length_hbm, finished_hbm, tokens_hbm, out, *scratch):
    plan, length, finished, tokens, send, sems = scratch
    pairs = [
        (plan_hbm, plan),
        (length_hbm, length),
        (finished_hbm, finished),
        (tokens_hbm, tokens),
    ]
    wait_all(start_all([pltpu.make_async_copy(*pair, sems.at[n]) for n, pair in enumerate(pairs)]))
    count = tokens.shape[0]
    shape = (send.shape[0], PARTS * count)
    row, col = iota(shape, 0), iota(shape, 1)
    source = col & (count - 1)
    wanted = by_index(row >> 3, send.shape[0] // 8, lambda d: plan[d])
    alive = by_index(source, count, alive_of(length, finished))
    chosen = (wanted == source) & ((row & 7) == (col >> 3)) & (alive > 0)
    chosen = jnp.where(chosen, 1.0, 0.0).astype(BF16)
    flat = sub_rows(tokens[...], send.shape[1])
    send[...] = jnp.dot(chosen, flat, preferred_element_type=F32).astype(BF16)
    wait_all(start_all([pltpu.make_async_copy(send, out, sems.at[0])]))


def routing_kernel(plan_hbm, length_hbm, finished_hbm, routes_hbm, score_hbm, *rest):
    scatter, gather, plan, length, finished, routes, score, sems = rest
    pairs = [
        (plan_hbm, plan),
        (length_hbm, length),
        (finished_hbm, finished),
        (routes_hbm, routes),
        (score_hbm, score),
    ]
    wait_all(start_all([pltpu.make_async_copy(*pair, sems.at[n]) for n, pair in enumerate(pairs)]))
    top, slots = routes.shape
    lanes = scatter.shape[0]
    experts = lanes // 8
    count = slots // 2
    names = jnp.transpose(routes[...].astype(F32))
    scores = jnp.transpose(score[...])
    expert = iota((slots, experts), 1).astype(F32)
    named = jnp.zeros((slots, experts), F32)
    weight = jnp.zeros((slots, experts), F32)
    for k in range(top):
        hit = names[:, k : k + 1] == expert
        named = jnp.where(hit, 1.0, named)
        weight = jnp.where(hit, scores[:, k : k + 1], weight)
    weight = 2.5 * weight / jnp.sum(scores, axis=1, keepdims=True)
    lower = jnp.where(iota((slots, slots), 1) < iota((slots, slots), 0), 1.0, 0.0).astype(BF16)
    position = jnp.dot(lower, named.astype(BF16), preferred_element_type=F32)
    high = weight.astype(BF16).astype(F32)
    low = weight - high
    stacked = jnp.concatenate([named, position, high, low], axis=0).astype(BF16)
    widen = iota((experts, lanes), 0) == (iota((experts, lanes), 1) >> 3)
    wide = jnp.dot(stacked, jnp.where(widen, 1.0, 0.0).astype(BF16), preferred_element_type=F32)
    lane = iota((slots, lanes), 1)
    part = lane & (PARTS - 1)
    place = ((lane >> 2) & 1).astype(F32)
    taken = (wide[:slots] > 0.5) & (wide[slots : 2 * slots] == place)
    taken = jnp.where(taken, 1.0, 0.0)

    row = iota((count, lanes), 0)
    alive = by_index(row, count, alive_of(length, finished))
    moved = jnp.zeros((count, lanes), jnp.int32)
    for d in range(count):
        moved = jnp.where(row == plan[d], 1, moved)
    stays = (alive > 0) & (moved == 0)
    half = part[:count]
    pieces = [jnp.where(stays & (half == q), taken[:count], 0.0) for q in range(PARTS)]
    for i in range(count):
        pieces.append(jnp.where(half == row, taken[count + i : count + i + 1], 0.0))
    used = len(pieces) * count
    pieces.append(jnp.zeros((scatter.shape[1] - used, lanes), F32))
    scatter[...] = jnp.transpose(jnp.concatenate(pieces, axis=0)).astype(BF16)

    pieces = []
    for start in (2 * slots, 3 * slots):
        wanted = wide[start : start + slots] * taken
        pieces += [jnp.where(part == q, wanted, 0.0) for q in range(PARTS)]
    gather[...] = jnp.concatenate(pieces, axis=0).astype(BF16)


def dispatch_kernel(scatter, tokens, arrived, out, block, sems):
    lanes, width = out.shape
    pad = scatter.shape[1] - PARTS * tokens.shape[0] - arrived.shape[0]
    pieces = [tokens[:, q * width : (q + 1) * width].astype(F32) for q in range(PARTS)]
    pieces += [arrived[...].astype(F32), jnp.zeros((pad, width), F32)]
    flat = jnp.concatenate(pieces, axis=0).astype(BF16)
    copies = []
    for b in range(lanes // 256):
        part = pl.ds(b * 256, 256)
        rows = jnp.dot(scatter[part, :], flat, preferred_element_type=F32)
        block[part, :] = rows.astype(BF16)
        copies += start_all([pltpu.make_async_copy(block.at[part], out.at[part], sems.at[b])])
    wait_all(copies)


def expert_kernel(recv, w_gate, w_up, w_down, out, *scratch):
    gates, ups, downs, rows, hidden, results, sent, sems = scratch
    width = recv.shape[1]
    blocks = recv.shape[0] // 256
    chunk = gates.shape[2]
    wide = [pl.ds(n * chunk, chunk) for n in range(gates.shape[0])]
    gate_copies = [
        pltpu.make_async_copy(w_gate.at[0, :, part], gates.at[n], sems.at[0, n])
        for n, part in enumerate(wide)
    ]
    up_copies = [
        pltpu.make_async_copy(w_up.at[0, :, part], ups.at[n], sems.at[1, n])
        for n, part in enumerate(wide)
    ]
    down_copies = [
        pltpu.make_async_copy(w_down.at[0, :, pl.ds(q * width, width)], downs.at[q], sems.at[2, q])
        for q in range(PARTS)
    ]
    for n in range(len(wide)):
        start_all([gate_copies[n], up_copies[n]])
    start_all(down_copies)

    one, two = iota((256, 256), 0), iota((256, 256), 1)
    apart = ((one & 63) * PARTS + (one >> 6)) == two
    together = ((two & 63) * PARTS + (two >> 6)) == one
    apart = jnp.where(apart, 1.0, 0.0).astype(BF16)
    together = jnp.where(together, 1.0, 0.0).astype(BF16)
    for b in range(blocks):
        got = jnp.dot(apart, recv[b * 256 : (b + 1) * 256, :], preferred_element_type=F32)
        got = got.astype(BF16)
        for q in range(PARTS):
            part = slice(q * width, (q + 1) * width)
            rows[b * 64 : (b + 1) * 64, part] = got[q * 64 : (q + 1) * 64, :]

    for n in range(len(wide)):
        gate_copies[n].wait()
        gate = jnp.dot(rows[...], gates[n], preferred_element_type=F32)
        up_copies[n].wait()
        up = jnp.dot(rows[...], ups[n], preferred_element_type=F32)
        value = gate / (1.0 + jnp.exp(-gate)) * up
        hidden[:, n * chunk : (n + 1) * chunk] = value.astype(BF16)
    for q in range(PARTS):
        down_copies[q].wait()
        result = jnp.dot(hidden[...], downs[q], preferred_element_type=F32).astype(BF16)
        for b in range(blocks):
            results[b, q * 64 : (q + 1) * 64, :] = result[b * 64 : (b + 1) * 64, :]
    copies = []
    for b in range(blocks):
        part = pl.ds(b * 256, 256)
        value = jnp.dot(together, results[b], preferred_element_type=F32).astype(BF16)
        sent[part, :] = value
        copies += start_all([pltpu.make_async_copy(sent.at[part], out.at[part], sems.at[0, b])])
    wait_all(copies)


def combine_kernel(gather, recv, out):
    slots = out.shape[0]
    width = recv.shape[1]
    summed = jnp.dot(gather[...], recv[...], preferred_element_type=F32)
    half = summed.shape[0] // 2
    summed = summed[:half] + summed[half:]
    for q in range(PARTS):
        out[:, q * width : (q + 1) * width] = summed[q * slots : (q + 1) * slots].astype(BF16)


def call(kernel, outs, in_specs, cost, scratch=(), limit=32, in_hbm=False):
    shape_of = pltpu.HBM if in_hbm else jax.ShapeDtypeStruct
    shapes = [shape_of(shape, BF16) for shape in outs]
    specs = [HBM if in_hbm else VMEM] * len(outs)
    return pl.pallas_call(
        kernel,
        out_shape=shapes if len(shapes) > 1 else shapes[0],
        in_specs=in_specs,
        out_specs=specs if len(specs) > 1 else specs[0],
        scratch_shapes=list(scratch),
        compiler_params=pltpu.CompilerParams(vmem_limit_bytes=limit * 2**20),
        cost_estimate=pl.CostEstimate(flops=cost[0], bytes_accessed=cost[1], transcendentals=0),
    )


def on_device(
    tokens,
    queries,
    latent_cache,
    new_latent,
    lengths,
    finished,
    migrate,
    routes,
    route_score,
    w_gate,
    w_up,
    w_down,
):
    count, model = tokens.shape
    slots = routes.shape[0]
    replicas = lax.axis_size("replica")
    devices = replicas * lax.axis_size("expert")
    width = model // PARTS
    lanes = devices * CAP * PARTS
    hidden = w_gate.shape[2]
    plan = migrate.reshape(replicas)

    def exchange(values):
        values = values.reshape(devices, 8, width)
        values = lax.all_to_all(values, BOTH, split_axis=0, concat_axis=0, tiled=True)
        return values.reshape(lanes, width)

    def in_hbm(*values):
        return [pltpu.with_memory_space_constraint(value, pltpu.HBM) for value in values]

    integers = [
        pltpu.SMEM((replicas,), jnp.int32),
        pltpu.SMEM((count,), jnp.int32),
        pltpu.SMEM((count,), jnp.int32),
    ]
    send = call(
        pick_kernel,
        [(replicas * 8, width)],
        [HBM] * 4,
        (10**6, 10**5),
        integers
        + [
            pltpu.VMEM((count, model), BF16),
            pltpu.VMEM((replicas * 8, width), BF16),
            pltpu.SemaphoreType.DMA((4,)),
        ],
        in_hbm=True,
    )(*in_hbm(plan, lengths, finished, tokens))
    arrived = lax.all_to_all(
        send.reshape(replicas, 8, width), "replica", split_axis=0, concat_axis=0, tiled=True
    ).reshape(replicas * 8, width)
    scatter, gather = call(
        routing_kernel,
        [(lanes, 128), (2 * PARTS * slots, lanes)],
        [HBM] * 5,
        (10**7, 10**6),
        integers
        + [
            pltpu.VMEM((routes.shape[1], slots), jnp.int32),
            pltpu.VMEM((routes.shape[1], slots), F32),
            pltpu.SemaphoreType.DMA((5,)),
        ],
    )(*in_hbm(plan, lengths, finished, routes.T, route_score.T))
    outgoing = call(
        dispatch_kernel,
        [(lanes, width)],
        [VMEM] * 3,
        (2 * 10**8, 2 * 10**6),
        [pltpu.VMEM((lanes, width), BF16), pltpu.SemaphoreType.DMA((lanes // 256,))],
        in_hbm=True,
    )(scatter, tokens, arrived)
    queries, outgoing = lax.optimization_barrier((queries, outgoing))
    incoming = exchange(outgoing)

    own_length = jnp.where(finished == 0, lengths, 0)
    attended = attend(queries, latent_cache, new_latent, own_length)
    sending = plan >= 0
    moved_out = jnp.any((plan[:, None] == jnp.arange(count)[None, :]), axis=0)
    leave = jnp.where(sending[:, None, None], attended[jnp.maximum(plan, 0)], jnp.zeros((), BF16))
    leave, incoming = lax.optimization_barrier((leave, incoming))
    landed = lax.all_to_all(leave, "replica", split_axis=0, concat_axis=0, tiled=True)
    stay = jnp.where(moved_out[:, None, None], jnp.zeros((), BF16), attended)
    attended_out = jnp.concatenate([stay, landed], axis=0).reshape(slots, HEADS * VDIM)

    results = call(
        expert_kernel,
        [(lanes, width)],
        [VMEM] + [HBM] * 3,
        (6 * devices * CAP * model * hidden, 6 * model * hidden),
        [
            pltpu.VMEM((4, model, hidden // 4), BF16),
            pltpu.VMEM((4, model, hidden // 4), BF16),
            pltpu.VMEM((PARTS, hidden, width), BF16),
            pltpu.VMEM((devices * CAP, model), BF16),
            pltpu.VMEM((devices * CAP, hidden), BF16),
            pltpu.VMEM((lanes // 256, 256, width), BF16),
            pltpu.VMEM((lanes, width), BF16),
            pltpu.SemaphoreType.DMA((3, 4)),
        ],
        46,
        True,
    )(incoming, *in_hbm(w_gate, w_up, w_down))
    returned = exchange(results)
    expert_out = call(combine_kernel, [(slots, model)], [VMEM] * 2, (2 * 10**8, 2 * 10**6))(
        gather, returned
    )
    return (attended_out, expert_out)


def solution(mesh):
    rows = P(BOTH, None)
    blocks = P(BOTH, None, None)
    flat = P(BOTH)
    return jax.shard_map(
        on_device,
        mesh=mesh,
        in_specs=(rows, rows, blocks, rows, flat, flat, blocks, rows, rows, blocks, blocks, blocks),
        out_specs=(rows, rows),
        check_vma=False,
    )
```

```python
import jax
import jax.numpy as jnp
from jax import lax
from jax.experimental import pallas as pl
from jax.experimental.pallas import tpu as pltpu
from jax.sharding import PartitionSpec as P

HEADS = 64
VDIM = 512
LAT = 576
BOTH = ("replica", "expert")
F32 = jnp.float32
BF16 = jnp.bfloat16

PARTS = 4
CAP = 2

score_scale = 192.0 ** (-0.5)

VMEM = pl.BlockSpec(memory_space=pltpu.VMEM)
SMEM = pl.BlockSpec(memory_space=pltpu.SMEM)
HBM = pl.BlockSpec(memory_space=pltpu.HBM)


def iota(shape, dim):
    return lax.broadcasted_iota(jnp.int32, shape, dim)


def attend(query_rows, latent_rows, own_latent, live_length):
    row_count = query_rows.shape[0]
    per_head = query_rows.reshape(row_count, HEADS, LAT)
    scores = (
        jnp.einsum("nhl,ntl->nht", per_head, latent_rows, preferred_element_type=F32) * score_scale
    )
    own_score = jnp.einsum("nhl,nl->nh", per_head, own_latent, preferred_element_type=F32)
    own_score = own_score * score_scale
    visible = iota((1, 1, latent_rows.shape[1]), 2) < live_length[:, None, None]
    scores = jnp.where(visible, scores, -jnp.inf)
    largest = jnp.maximum(jnp.max(scores, axis=2), own_score)
    weights = jnp.exp(scores - largest[:, :, None])
    own_weight = jnp.exp(own_score - largest)
    denominator = jnp.sum(weights, axis=2) + own_weight
    context = jnp.einsum(
        "nht,ntv->nhv",
        weights.astype(BF16),
        latent_rows[:, :, :VDIM],
        preferred_element_type=F32,
    )
    own_rounded = lax.optimization_barrier(own_weight.astype(BF16)).astype(F32)
    context = context + own_rounded[:, :, None] * own_latent[:, None, :VDIM].astype(F32)
    normalized = context / denominator[:, :, None] * (live_length > 0).astype(F32)[:, None, None]
    return normalized.astype(BF16)


def by_index(index, count, value_of):
    spread = jnp.zeros(index.shape, jnp.int32)
    for i in range(count):
        spread = jnp.where(index == i, value_of(i), spread)
    return spread


def alive_of(length, finished):
    return lambda s: jnp.where(finished[s] == 0, length[s], 0)


def start_all(copies):
    for copy in copies:
        copy.start()
    return copies


def wait_all(copies):
    for copy in copies:
        copy.wait()


def sub_rows(rows, width):
    pieces = [rows[:, q * width : (q + 1) * width].astype(F32) for q in range(PARTS)]
    return jnp.concatenate(pieces, axis=0).astype(BF16)


def pick_kernel(plan_hbm, length_hbm, finished_hbm, tokens_hbm, out, *scratch):
    plan, length, finished, tokens, send, sems = scratch
    pairs = [
        (plan_hbm, plan),
        (length_hbm, length),
        (finished_hbm, finished),
        (tokens_hbm, tokens),
    ]
    wait_all(start_all([pltpu.make_async_copy(*pair, sems.at[n]) for n, pair in enumerate(pairs)]))
    count = tokens.shape[0]
    shape = (send.shape[0], PARTS * count)
    row, col = iota(shape, 0), iota(shape, 1)
    source = col & (count - 1)
    wanted = by_index(row >> 3, send.shape[0] // 8, lambda d: plan[d])
    alive = by_index(source, count, alive_of(length, finished))
    chosen = (wanted == source) & ((row & 7) == (col >> 3)) & (alive > 0)
    chosen = jnp.where(chosen, 1.0, 0.0).astype(BF16)
    flat = sub_rows(tokens[...], send.shape[1])
    send[...] = jnp.dot(chosen, flat, preferred_element_type=F32).astype(BF16)
    wait_all(start_all([pltpu.make_async_copy(send, out, sems.at[0])]))


def routing_kernel(plan_hbm, length_hbm, finished_hbm, routes_hbm, score_hbm, tokens_hbm, *rest):
    scatter, gather, flat, plan, length, finished, routes, score, tokens, sems = rest
    pairs = [
        (plan_hbm, plan),
        (length_hbm, length),
        (finished_hbm, finished),
        (routes_hbm, routes),
        (score_hbm, score),
        (tokens_hbm, tokens),
    ]
    wait_all(start_all([pltpu.make_async_copy(*pair, sems.at[n]) for n, pair in enumerate(pairs)]))
    flat[...] = sub_rows(tokens[...], flat.shape[1])
    top, slots = routes.shape
    lanes = scatter.shape[0]
    experts = lanes // 8
    count = slots // 2
    names = jnp.transpose(routes[...].astype(F32))
    scores = jnp.transpose(score[...])
    expert = iota((slots, experts), 1).astype(F32)
    named = jnp.zeros((slots, experts), F32)
    weight = jnp.zeros((slots, experts), F32)
    for k in range(top):
        hit = names[:, k : k + 1] == expert
        named = jnp.where(hit, 1.0, named)
        weight = jnp.where(hit, scores[:, k : k + 1], weight)
    weight = 2.5 * weight / jnp.sum(scores, axis=1, keepdims=True)
    lower = jnp.where(iota((slots, slots), 1) < iota((slots, slots), 0), 1.0, 0.0).astype(BF16)
    position = jnp.dot(lower, named.astype(BF16), preferred_element_type=F32)
    high = weight.astype(BF16).astype(F32)
    low = weight - high
    stacked = jnp.concatenate([named, position, high, low], axis=0).astype(BF16)
    widen = iota((experts, lanes), 0) == (iota((experts, lanes), 1) >> 3)
    wide = jnp.dot(stacked, jnp.where(widen, 1.0, 0.0).astype(BF16), preferred_element_type=F32)
    lane = iota((slots, lanes), 1)
    part = lane & (PARTS - 1)
    place = ((lane >> 2) & 1).astype(F32)
    taken = (wide[:slots] > 0.5) & (wide[slots : 2 * slots] == place)
    taken = jnp.where(taken, 1.0, 0.0)

    row = iota((count, lanes), 0)
    alive = by_index(row, count, alive_of(length, finished))
    moved = jnp.zeros((count, lanes), jnp.int32)
    for d in range(count):
        moved = jnp.where(row == plan[d], 1, moved)
    stays = (alive > 0) & (moved == 0)
    half = part[:count]
    pieces = [jnp.where(stays & (half == q), taken[:count], 0.0) for q in range(PARTS)]
    for i in range(count):
        pieces.append(jnp.where(half == row, taken[count + i : count + i + 1], 0.0))
    used = len(pieces) * count
    pieces.append(jnp.zeros((scatter.shape[1] - used, lanes), F32))
    scatter[...] = jnp.transpose(jnp.concatenate(pieces, axis=0)).astype(BF16)

    pieces = []
    for start in (2 * slots, 3 * slots):
        wanted = wide[start : start + slots] * taken
        pieces += [jnp.where(part == q, wanted, 0.0) for q in range(PARTS)]
    gather[...] = jnp.concatenate(pieces, axis=0).astype(BF16)


def dispatch_kernel(scatter, tokens, arrived, out, block, sems):
    lanes, width = out.shape
    pad = scatter.shape[1] - tokens.shape[0] - arrived.shape[0]
    flat = jnp.concatenate([tokens[...], arrived[...], jnp.zeros((pad, width), BF16)], axis=0)
    copies = []
    for b in range(lanes // 256):
        part = pl.ds(b * 256, 256)
        rows = jnp.dot(scatter[part, :], flat, preferred_element_type=F32)
        block[part, :] = rows.astype(BF16)
        copies += start_all([pltpu.make_async_copy(block.at[part], out.at[part], sems.at[b])])
    wait_all(copies)


def expert_kernel(recv, w_gate, w_up, w_down, out, *scratch):
    gates, ups, downs, rows, hidden, partial, results, sent, sems = scratch
    width = recv.shape[1]
    blocks = recv.shape[0] // 256
    half = downs.shape[1]
    gate_copies, up_copies, down_copies = [], [], []
    for q in range(PARTS):
        part = pl.ds(q * width, width)
        gate_copies.append(pltpu.make_async_copy(w_gate.at[0, part, :], gates.at[q], sems.at[0, q]))
        up_copies.append(pltpu.make_async_copy(w_up.at[0, part, :], ups.at[q], sems.at[1, q]))
        start_all([gate_copies[q], up_copies[q]])
    for n in range(downs.shape[0]):
        part = pl.ds(n * half, half)
        down_copies.append(pltpu.make_async_copy(w_down.at[0, part, :], downs.at[n], sems.at[2, n]))
    start_all(down_copies)

    one, two = iota((256, 256), 0), iota((256, 256), 1)
    apart = ((one & 63) * PARTS + (one >> 6)) == two
    together = ((two & 63) * PARTS + (two >> 6)) == one
    apart = jnp.where(apart, 1.0, 0.0).astype(BF16)
    together = jnp.where(together, 1.0, 0.0).astype(BF16)
    for b in range(blocks):
        got = jnp.dot(apart, recv[b * 256 : (b + 1) * 256, :], preferred_element_type=F32)
        got = got.astype(BF16)
        for q in range(PARTS):
            rows[q, b * 64 : (b + 1) * 64, :] = got[q * 64 : (q + 1) * 64, :]

    gate = up = None
    for q in range(PARTS):
        gate_copies[q].wait()
        more = jnp.dot(rows[q], gates[q], preferred_element_type=F32)
        gate = more if gate is None else gate + more
        up_copies[q].wait()
        more = jnp.dot(rows[q], ups[q], preferred_element_type=F32)
        up = more if up is None else up + more
    hidden[...] = (gate / (1.0 + jnp.exp(-gate)) * up).astype(BF16)
    down_copies[0].wait()
    for q in range(PARTS):
        part = slice(q * width, (q + 1) * width)
        partial[q] = jnp.dot(hidden[:, :half], downs[0, :, part], preferred_element_type=F32)
    down_copies[1].wait()
    for q in range(PARTS):
        part = slice(q * width, (q + 1) * width)
        result = jnp.dot(hidden[:, half:], downs[1, :, part], preferred_element_type=F32)
        result = (partial[q] + result).astype(BF16)
        for b in range(blocks):
            results[b, q * 64 : (q + 1) * 64, :] = result[b * 64 : (b + 1) * 64, :]
    copies = []
    for b in range(blocks):
        part = pl.ds(b * 256, 256)
        value = jnp.dot(together, results[b], preferred_element_type=F32).astype(BF16)
        sent[part, :] = value
        copies += start_all([pltpu.make_async_copy(sent.at[part], out.at[part], sems.at[0, b])])
    wait_all(copies)


def combine_kernel(gather, recv, out):
    slots = out.shape[0]
    width = recv.shape[1]
    summed = jnp.dot(gather[...], recv[...], preferred_element_type=F32)
    half = summed.shape[0] // 2
    summed = summed[:half] + summed[half:]
    for q in range(PARTS):
        out[:, q * width : (q + 1) * width] = summed[q * slots : (q + 1) * slots].astype(BF16)


def call(kernel, outs, in_specs, cost, scratch=(), limit=32, in_hbm=False):
    shape_of = pltpu.HBM if in_hbm else jax.ShapeDtypeStruct
    shapes = [shape_of(shape, BF16) for shape in outs]
    specs = [HBM if in_hbm else VMEM] * len(outs)
    return pl.pallas_call(
        kernel,
        out_shape=shapes if len(shapes) > 1 else shapes[0],
        in_specs=in_specs,
        out_specs=specs if len(specs) > 1 else specs[0],
        scratch_shapes=list(scratch),
        compiler_params=pltpu.CompilerParams(vmem_limit_bytes=limit * 2**20),
        cost_estimate=pl.CostEstimate(flops=cost[0], bytes_accessed=cost[1], transcendentals=0),
    )


def on_device(
    tokens,
    queries,
    latent_cache,
    new_latent,
    lengths,
    finished,
    migrate,
    routes,
    route_score,
    w_gate,
    w_up,
    w_down,
):
    count, model = tokens.shape
    slots = routes.shape[0]
    replicas = lax.axis_size("replica")
    devices = replicas * lax.axis_size("expert")
    width = model // PARTS
    lanes = devices * CAP * PARTS
    hidden = w_gate.shape[2]
    plan = migrate.reshape(replicas)

    def exchange(values):
        values = values.reshape(devices, 8, width)
        values = lax.all_to_all(values, BOTH, split_axis=0, concat_axis=0, tiled=True)
        return values.reshape(lanes, width)

    def in_hbm(*values):
        return [pltpu.with_memory_space_constraint(value, pltpu.HBM) for value in values]

    integers = [
        pltpu.SMEM((replicas,), jnp.int32),
        pltpu.SMEM((count,), jnp.int32),
        pltpu.SMEM((count,), jnp.int32),
    ]
    send = call(
        pick_kernel,
        [(replicas * 8, width)],
        [HBM] * 4,
        (10**6, 10**5),
        integers
        + [
            pltpu.VMEM((count, model), BF16),
            pltpu.VMEM((replicas * 8, width), BF16),
            pltpu.SemaphoreType.DMA((4,)),
        ],
        in_hbm=True,
    )(*in_hbm(plan, lengths, finished, tokens))
    arrived = lax.all_to_all(
        send.reshape(replicas, 8, width), "replica", split_axis=0, concat_axis=0, tiled=True
    ).reshape(replicas * 8, width)
    scatter, gather, flat = call(
        routing_kernel,
        [(lanes, 128), (2 * PARTS * slots, lanes), (PARTS * count, width)],
        [HBM] * 6,
        (10**7, 10**6),
        integers
        + [
            pltpu.VMEM((routes.shape[1], slots), jnp.int32),
            pltpu.VMEM((routes.shape[1], slots), F32),
            pltpu.VMEM((count, model), BF16),
            pltpu.SemaphoreType.DMA((6,)),
        ],
    )(*in_hbm(plan, lengths, finished, routes.T, route_score.T, tokens))
    outgoing = call(
        dispatch_kernel,
        [(lanes, width)],
        [VMEM] * 3,
        (2 * 10**8, 2 * 10**6),
        [pltpu.VMEM((lanes, width), BF16), pltpu.SemaphoreType.DMA((lanes // 256,))],
        in_hbm=True,
    )(scatter, flat, arrived)
    held = (queries, latent_cache, new_latent, lengths, finished, plan, outgoing)
    held = lax.optimization_barrier(held)
    queries, latent_cache, new_latent, lengths, finished, plan, outgoing = held
    incoming = exchange(outgoing)

    own_length = jnp.where(finished == 0, lengths, 0)
    attended = attend(queries, latent_cache, new_latent, own_length)
    sending = plan >= 0
    moved_out = jnp.any((plan[:, None] == jnp.arange(count)[None, :]), axis=0)
    leave = jnp.where(sending[:, None, None], attended[jnp.maximum(plan, 0)], jnp.zeros((), BF16))
    leave, incoming = lax.optimization_barrier((leave, incoming))
    landed = lax.all_to_all(leave, "replica", split_axis=0, concat_axis=0, tiled=True)
    stay = jnp.where(moved_out[:, None, None], jnp.zeros((), BF16), attended)
    attended_out = jnp.concatenate([stay, landed], axis=0).reshape(slots, HEADS * VDIM)

    results = call(
        expert_kernel,
        [(lanes, width)],
        [VMEM] + [HBM] * 3,
        (6 * devices * CAP * model * hidden, 6 * model * hidden),
        [
            pltpu.VMEM((PARTS, width, hidden), BF16),
            pltpu.VMEM((PARTS, width, hidden), BF16),
            pltpu.VMEM((2, hidden // 2, model), BF16),
            pltpu.VMEM((PARTS, devices * CAP, width), BF16),
            pltpu.VMEM((devices * CAP, hidden), BF16),
            pltpu.VMEM((PARTS, devices * CAP, width), F32),
            pltpu.VMEM((lanes // 256, 256, width), BF16),
            pltpu.VMEM((lanes, width), BF16),
            pltpu.SemaphoreType.DMA((3, 4)),
        ],
        46,
        True,
    )(incoming, *in_hbm(w_gate, w_up, w_down))
    returned = exchange(results)
    expert_out = call(combine_kernel, [(slots, model)], [VMEM] * 2, (2 * 10**8, 2 * 10**6))(
        gather, returned
    )
    return (attended_out, expert_out)


def solution(mesh):
    rows = P(BOTH, None)
    blocks = P(BOTH, None, None)
    flat = P(BOTH)
    return jax.shard_map(
        on_device,
        mesh=mesh,
        in_specs=(rows, rows, blocks, rows, flat, flat, blocks, rows, rows, blocks, blocks, blocks),
        out_specs=(rows, rows),
        check_vma=False,
    )
```

```python
import jax
import jax.numpy as jnp
from jax import lax
from jax.experimental import pallas as pl
from jax.experimental.pallas import tpu as pltpu
from jax.sharding import PartitionSpec as P

HEADS = 64
VDIM = 512
LAT = 576
BOTH = ("replica", "expert")
F32 = jnp.float32
BF16 = jnp.bfloat16

PARTS = 4
CAP = 2

score_scale = 192.0 ** (-0.5)

VMEM = pl.BlockSpec(memory_space=pltpu.VMEM)
SMEM = pl.BlockSpec(memory_space=pltpu.SMEM)
HBM = pl.BlockSpec(memory_space=pltpu.HBM)


def iota(shape, dim):
    return lax.broadcasted_iota(jnp.int32, shape, dim)


def attend(query_rows, latent_rows, own_latent, live_length):
    row_count = query_rows.shape[0]
    per_head = query_rows.reshape(row_count, HEADS, LAT)
    scores = (
        jnp.einsum("nhl,ntl->nht", per_head, latent_rows, preferred_element_type=F32) * score_scale
    )
    own_score = jnp.einsum("nhl,nl->nh", per_head, own_latent, preferred_element_type=F32)
    own_score = own_score * score_scale
    visible = iota((1, 1, latent_rows.shape[1]), 2) < live_length[:, None, None]
    scores = jnp.where(visible, scores, -jnp.inf)
    largest = jnp.maximum(jnp.max(scores, axis=2), own_score)
    weights = jnp.exp(scores - largest[:, :, None])
    own_weight = jnp.exp(own_score - largest)
    denominator = jnp.sum(weights, axis=2) + own_weight
    context = jnp.einsum(
        "nht,ntv->nhv",
        weights.astype(BF16),
        latent_rows[:, :, :VDIM],
        preferred_element_type=F32,
    )
    own_rounded = lax.optimization_barrier(own_weight.astype(BF16)).astype(F32)
    context = context + own_rounded[:, :, None] * own_latent[:, None, :VDIM].astype(F32)
    normalized = context / denominator[:, :, None] * (live_length > 0).astype(F32)[:, None, None]
    return normalized.astype(BF16)


def by_index(index, count, value_of):
    spread = jnp.zeros(index.shape, jnp.int32)
    for i in range(count):
        spread = jnp.where(index == i, value_of(i), spread)
    return spread


def alive_of(length, finished):
    return lambda s: jnp.where(finished[s] == 0, length[s], 0)


def start_all(copies):
    for copy in copies:
        copy.start()
    return copies


def wait_all(copies):
    for copy in copies:
        copy.wait()


def sub_rows(rows, width):
    pieces = [rows[:, q * width : (q + 1) * width].astype(F32) for q in range(PARTS)]
    return jnp.concatenate(pieces, axis=0).astype(BF16)


def pick_kernel(plan_hbm, length_hbm, finished_hbm, tokens_hbm, out, *scratch):
    plan, length, finished, tokens, send, sems = scratch
    pairs = [
        (plan_hbm, plan),
        (length_hbm, length),
        (finished_hbm, finished),
        (tokens_hbm, tokens),
    ]
    wait_all(start_all([pltpu.make_async_copy(*pair, sems.at[n]) for n, pair in enumerate(pairs)]))
    count = tokens.shape[0]
    shape = (send.shape[0], PARTS * count)
    row, col = iota(shape, 0), iota(shape, 1)
    source = col & (count - 1)
    wanted = by_index(row >> 3, send.shape[0] // 8, lambda d: plan[d])
    alive = by_index(source, count, alive_of(length, finished))
    chosen = (wanted == source) & ((row & 7) == (col >> 3)) & (alive > 0)
    chosen = jnp.where(chosen, 1.0, 0.0).astype(BF16)
    flat = sub_rows(tokens[...], send.shape[1])
    send[...] = jnp.dot(chosen, flat, preferred_element_type=F32).astype(BF16)
    wait_all(start_all([pltpu.make_async_copy(send, out, sems.at[0])]))


def routing_kernel(plan_hbm, length_hbm, finished_hbm, routes_hbm, score_hbm, tokens_hbm, *rest):
    scatter, gather, flat, plan, length, finished, routes, score, tokens, sems = rest
    pairs = [
        (plan_hbm, plan),
        (length_hbm, length),
        (finished_hbm, finished),
        (routes_hbm, routes),
        (score_hbm, score),
        (tokens_hbm, tokens),
    ]
    wait_all(start_all([pltpu.make_async_copy(*pair, sems.at[n]) for n, pair in enumerate(pairs)]))
    flat[...] = sub_rows(tokens[...], flat.shape[1])
    top, slots = routes.shape
    lanes = scatter.shape[0]
    experts = lanes // 8
    count = slots // 2
    names = jnp.transpose(routes[...].astype(F32))
    scores = jnp.transpose(score[...])
    expert = iota((slots, experts), 1).astype(F32)
    named = jnp.zeros((slots, experts), F32)
    weight = jnp.zeros((slots, experts), F32)
    for k in range(top):
        hit = names[:, k : k + 1] == expert
        named = jnp.where(hit, 1.0, named)
        weight = jnp.where(hit, scores[:, k : k + 1], weight)
    weight = 2.5 * weight / jnp.sum(scores, axis=1, keepdims=True)
    lower = jnp.where(iota((slots, slots), 1) < iota((slots, slots), 0), 1.0, 0.0).astype(BF16)
    position = jnp.dot(lower, named.astype(BF16), preferred_element_type=F32)
    high = weight.astype(BF16).astype(F32)
    low = weight - high
    stacked = jnp.concatenate([named, position, high, low], axis=0).astype(BF16)
    widen = iota((experts, lanes), 0) == (iota((experts, lanes), 1) >> 3)
    wide = jnp.dot(stacked, jnp.where(widen, 1.0, 0.0).astype(BF16), preferred_element_type=F32)
    lane = iota((slots, lanes), 1)
    part = lane & (PARTS - 1)
    place = ((lane >> 2) & 1).astype(F32)
    taken = (wide[:slots] > 0.5) & (wide[slots : 2 * slots] == place)
    taken = jnp.where(taken, 1.0, 0.0)

    row = iota((count, lanes), 0)
    alive = by_index(row, count, alive_of(length, finished))
    moved = jnp.zeros((count, lanes), jnp.int32)
    for d in range(count):
        moved = jnp.where(row == plan[d], 1, moved)
    stays = (alive > 0) & (moved == 0)
    half = part[:count]
    pieces = [jnp.where(stays & (half == q), taken[:count], 0.0) for q in range(PARTS)]
    for i in range(count):
        pieces.append(jnp.where(half == row, taken[count + i : count + i + 1], 0.0))
    used = len(pieces) * count
    pieces.append(jnp.zeros((scatter.shape[1] - used, lanes), F32))
    scatter[...] = jnp.transpose(jnp.concatenate(pieces, axis=0)).astype(BF16)

    pieces = []
    for start in (2 * slots, 3 * slots):
        wanted = wide[start : start + slots] * taken
        pieces += [jnp.where(part == q, wanted, 0.0) for q in range(PARTS)]
    gather[...] = jnp.concatenate(pieces, axis=0).astype(BF16)


def dispatch_kernel(scatter, tokens, arrived, out, block, sems):
    lanes, width = out.shape
    pad = scatter.shape[1] - tokens.shape[0] - arrived.shape[0]
    flat = jnp.concatenate([tokens[...], arrived[...], jnp.zeros((pad, width), BF16)], axis=0)
    copies = []
    for b in range(lanes // 256):
        part = pl.ds(b * 256, 256)
        rows = jnp.dot(scatter[part, :], flat, preferred_element_type=F32)
        block[part, :] = rows.astype(BF16)
        copies += start_all([pltpu.make_async_copy(block.at[part], out.at[part], sems.at[b])])
    wait_all(copies)


def one_hot(hit):
    return jnp.where(hit, 1.0, 0.0).astype(BF16)


def expert_kernel(recv, w_gate, w_up, w_down, out, *scratch):
    gates, ups, downs, rows, results, sent, sems = scratch
    lanes, width = recv.shape
    blocks = lanes // 256
    total = lanes // PARTS
    gate_copies, up_copies, down_copies = [], [], []
    for q in range(PARTS):
        part = pl.ds(q * width, width)
        gate_copies.append(pltpu.make_async_copy(w_gate.at[0, part, :], gates.at[q], sems.at[0, q]))
        up_copies.append(pltpu.make_async_copy(w_up.at[0, part, :], ups.at[q], sems.at[1, q]))
        down_copies.append(
            pltpu.make_async_copy(w_down.at[0, :, part], downs.at[q], sems.at[2, q])
        )
        start_all([gate_copies[q], up_copies[q]])
    start_all(down_copies)

    one, two = iota((256, 256), 0), iota((256, 256), 1)
    apart = one_hot(((one & 63) * PARTS + (one >> 6)) == two)
    together = one_hot(((two & 63) * PARTS + (two >> 6)) == one)
    used = jnp.zeros((8, total), F32)
    for b in range(blocks):
        part = recv[b * 256 : (b + 1) * 256, :]
        nonzero = jnp.where(part.astype(F32) != 0, 1.0, 0.0).astype(BF16)
        found = lax.dot_general(
            jnp.ones((8, width), BF16),
            nonzero,
            (((1,), (1,)), ((), ())),
            preferred_element_type=F32,
        )
        found = jnp.where(found > 0, 1.0, 0.0).astype(BF16)
        pool = one_hot((iota((256, total), 0) >> 2) + b * 64 == iota((256, total), 1))
        used = used + jnp.dot(found, pool, preferred_element_type=F32)
        got = jnp.dot(apart, part, preferred_element_type=F32).astype(BF16)
        for q in range(PARTS):
            rows[q, b * 64 : (b + 1) * 64, :] = got[q * 64 : (q + 1) * 64, :]
    used = jnp.where(used > 0, 1.0, 0.0)
    before = one_hot(iota((total, total), 0) < iota((total, total), 1))
    place = jnp.dot(used.astype(BF16), before, preferred_element_type=F32)
    count = jnp.sum(used[:1, :]).astype(jnp.int32)

    def body(size):
        pick = (iota((size, total), 0).astype(F32) == place[:1, :]) & (used[:1, :] > 0)
        pick = jnp.where(pick, 1.0, 0.0)
        spread = jnp.transpose(pick).astype(BF16)
        pick = pick.astype(BF16)
        packed = [
            jnp.dot(pick, rows[q], preferred_element_type=F32).astype(BF16) for q in range(PARTS)
        ]
        gate = up = None
        for q in range(PARTS):
            gate_copies[q].wait()
            more = jnp.dot(packed[q], gates[q], preferred_element_type=F32)
            gate = more if gate is None else gate + more
            up_copies[q].wait()
            more = jnp.dot(packed[q], ups[q], preferred_element_type=F32)
            up = more if up is None else up + more
        hidden = (gate / (1.0 + jnp.exp(-gate)) * up).astype(BF16)
        for q in range(PARTS):
            down_copies[q].wait()
            result = jnp.dot(hidden, downs[q], preferred_element_type=F32).astype(BF16)
            result = jnp.dot(spread, result, preferred_element_type=F32).astype(BF16)
            for b in range(blocks):
                results[b, q * 64 : (q + 1) * 64, :] = result[b * 64 : (b + 1) * 64, :]

    small = 160

    @pl.when(count <= small)
    def _():
        body(small)

    @pl.when(count > small)
    def _():
        body(total)

    copies = []
    for b in range(blocks):
        part = pl.ds(b * 256, 256)
        value = jnp.dot(together, results[b], preferred_element_type=F32).astype(BF16)
        sent[part, :] = value
        copies += start_all([pltpu.make_async_copy(sent.at[part], out.at[part], sems.at[0, b])])
    wait_all(copies)


def combine_kernel(gather, recv, out):
    slots = out.shape[0]
    width = recv.shape[1]
    summed = jnp.dot(gather[...], recv[...], preferred_element_type=F32)
    half = summed.shape[0] // 2
    summed = summed[:half] + summed[half:]
    for q in range(PARTS):
        out[:, q * width : (q + 1) * width] = summed[q * slots : (q + 1) * slots].astype(BF16)


def call(kernel, outs, in_specs, cost, scratch=(), limit=32, in_hbm=False):
    shape_of = pltpu.HBM if in_hbm else jax.ShapeDtypeStruct
    shapes = [shape_of(shape, BF16) for shape in outs]
    specs = [HBM if in_hbm else VMEM] * len(outs)
    return pl.pallas_call(
        kernel,
        out_shape=shapes if len(shapes) > 1 else shapes[0],
        in_specs=in_specs,
        out_specs=specs if len(specs) > 1 else specs[0],
        scratch_shapes=list(scratch),
        compiler_params=pltpu.CompilerParams(vmem_limit_bytes=limit * 2**20),
        cost_estimate=pl.CostEstimate(flops=cost[0], bytes_accessed=cost[1], transcendentals=0),
    )


def on_device(
    tokens,
    queries,
    latent_cache,
    new_latent,
    lengths,
    finished,
    migrate,
    routes,
    route_score,
    w_gate,
    w_up,
    w_down,
):
    count, model = tokens.shape
    slots = routes.shape[0]
    replicas = lax.axis_size("replica")
    devices = replicas * lax.axis_size("expert")
    width = model // PARTS
    lanes = devices * CAP * PARTS
    hidden = w_gate.shape[2]
    plan = migrate.reshape(replicas)

    def exchange(values):
        values = values.reshape(devices, 8, width)
        values = lax.all_to_all(values, BOTH, split_axis=0, concat_axis=0, tiled=True)
        return values.reshape(lanes, width)

    def in_hbm(*values):
        return [pltpu.with_memory_space_constraint(value, pltpu.HBM) for value in values]

    integers = [
        pltpu.SMEM((replicas,), jnp.int32),
        pltpu.SMEM((count,), jnp.int32),
        pltpu.SMEM((count,), jnp.int32),
    ]
    send = call(
        pick_kernel,
        [(replicas * 8, width)],
        [HBM] * 4,
        (10**6, 10**5),
        integers
        + [
            pltpu.VMEM((count, model), BF16),
            pltpu.VMEM((replicas * 8, width), BF16),
            pltpu.SemaphoreType.DMA((4,)),
        ],
        in_hbm=True,
    )(*in_hbm(plan, lengths, finished, tokens))
    arrived = lax.all_to_all(
        send.reshape(replicas, 8, width), "replica", split_axis=0, concat_axis=0, tiled=True
    ).reshape(replicas * 8, width)
    scatter, gather, flat = call(
        routing_kernel,
        [(lanes, 128), (2 * PARTS * slots, lanes), (PARTS * count, width)],
        [HBM] * 6,
        (10**7, 10**6),
        integers
        + [
            pltpu.VMEM((routes.shape[1], slots), jnp.int32),
            pltpu.VMEM((routes.shape[1], slots), F32),
            pltpu.VMEM((count, model), BF16),
            pltpu.SemaphoreType.DMA((6,)),
        ],
    )(*in_hbm(plan, lengths, finished, routes.T, route_score.T, tokens))
    outgoing = call(
        dispatch_kernel,
        [(lanes, width)],
        [VMEM] * 3,
        (2 * 10**8, 2 * 10**6),
        [pltpu.VMEM((lanes, width), BF16), pltpu.SemaphoreType.DMA((lanes // 256,))],
        in_hbm=True,
    )(scatter, flat, arrived)
    own_length = jnp.where(finished == 0, lengths, 0)
    held = lax.optimization_barrier((queries, latent_cache, new_latent, plan, outgoing))
    queries, latent_cache, new_latent, plan, outgoing = held
    incoming = exchange(outgoing)

    attended = attend(queries, latent_cache, new_latent, own_length)
    sending = plan >= 0
    moved_out = jnp.any((plan[:, None] == jnp.arange(count)[None, :]), axis=0)
    leave = jnp.where(sending[:, None, None], attended[jnp.maximum(plan, 0)], jnp.zeros((), BF16))
    leave, incoming = lax.optimization_barrier((leave, incoming))
    landed = lax.all_to_all(leave, "replica", split_axis=0, concat_axis=0, tiled=True)
    stay = jnp.where(moved_out[:, None, None], jnp.zeros((), BF16), attended)
    attended_out = jnp.concatenate([stay, landed], axis=0).reshape(slots, HEADS * VDIM)

    results = call(
        expert_kernel,
        [(lanes, width)],
        [VMEM] + [HBM] * 3,
        (6 * devices * CAP * model * hidden, 6 * model * hidden),
        [
            pltpu.VMEM((PARTS, width, hidden), BF16),
            pltpu.VMEM((PARTS, width, hidden), BF16),
            pltpu.VMEM((PARTS, hidden, width), BF16),
            pltpu.VMEM((PARTS, devices * CAP, width), BF16),
            pltpu.VMEM((lanes // 256, 256, width), BF16),
            pltpu.VMEM((lanes, width), BF16),
            pltpu.SemaphoreType.DMA((3, 4)),
        ],
        46,
        True,
    )(incoming, *in_hbm(w_gate, w_up, w_down))
    returned = exchange(results)
    expert_out = call(combine_kernel, [(slots, model)], [VMEM] * 2, (2 * 10**8, 2 * 10**6))(
        gather, returned
    )
    return (attended_out, expert_out)


def solution(mesh):
    rows = P(BOTH, None)
    blocks = P(BOTH, None, None)
    flat = P(BOTH)
    return jax.shard_map(
        on_device,
        mesh=mesh,
        in_specs=(rows, rows, blocks, rows, flat, flat, blocks, rows, rows, blocks, blocks, blocks),
        out_specs=(rows, rows),
        check_vma=False,
    )
```

```python
import jax
import jax.numpy as jnp
from jax import lax
from jax.experimental import pallas as pl
from jax.experimental.pallas import tpu as pltpu
from jax.sharding import PartitionSpec as P

HEADS = 64
VDIM = 512
LAT = 576
BOTH = ("replica", "expert")
F32 = jnp.float32
BF16 = jnp.bfloat16

PARTS = 4
CAP = 2

score_scale = 192.0 ** (-0.5)

VMEM = pl.BlockSpec(memory_space=pltpu.VMEM)
SMEM = pl.BlockSpec(memory_space=pltpu.SMEM)
HBM = pl.BlockSpec(memory_space=pltpu.HBM)


def iota(shape, dim):
    return lax.broadcasted_iota(jnp.int32, shape, dim)


def attend(query_rows, latent_rows, own_latent, live_length):
    row_count = query_rows.shape[0]
    per_head = query_rows.reshape(row_count, HEADS, LAT)
    scores = (
        jnp.einsum("nhl,ntl->nht", per_head, latent_rows, preferred_element_type=F32) * score_scale
    )
    own_score = jnp.einsum("nhl,nl->nh", per_head, own_latent, preferred_element_type=F32)
    own_score = own_score * score_scale
    visible = iota((1, 1, latent_rows.shape[1]), 2) < live_length[:, None, None]
    scores = jnp.where(visible, scores, -jnp.inf)
    largest = jnp.maximum(jnp.max(scores, axis=2), own_score)
    weights = jnp.exp(scores - largest[:, :, None])
    own_weight = jnp.exp(own_score - largest)
    denominator = jnp.sum(weights, axis=2) + own_weight
    context = jnp.einsum(
        "nht,ntv->nhv",
        weights.astype(BF16),
        latent_rows[:, :, :VDIM],
        preferred_element_type=F32,
    )
    own_rounded = lax.optimization_barrier(own_weight.astype(BF16)).astype(F32)
    context = context + own_rounded[:, :, None] * own_latent[:, None, :VDIM].astype(F32)
    normalized = context / denominator[:, :, None] * (live_length > 0).astype(F32)[:, None, None]
    return normalized.astype(BF16)


def by_index(index, count, value_of):
    spread = jnp.zeros(index.shape, jnp.int32)
    for i in range(count):
        spread = jnp.where(index == i, value_of(i), spread)
    return spread


def alive_of(length, finished):
    return lambda s: jnp.where(finished[s] == 0, length[s], 0)


def start_all(copies):
    for copy in copies:
        copy.start()
    return copies


def wait_all(copies):
    for copy in copies:
        copy.wait()


def sub_rows(rows, width):
    pieces = [rows[:, q * width : (q + 1) * width].astype(F32) for q in range(PARTS)]
    return jnp.concatenate(pieces, axis=0).astype(BF16)


def pick_kernel(plan_hbm, length_hbm, finished_hbm, tokens_hbm, out, *scratch):
    plan, length, finished, tokens, send, sems = scratch
    pairs = [
        (plan_hbm, plan),
        (length_hbm, length),
        (finished_hbm, finished),
        (tokens_hbm, tokens),
    ]
    wait_all(start_all([pltpu.make_async_copy(*pair, sems.at[n]) for n, pair in enumerate(pairs)]))
    count = tokens.shape[0]
    shape = (send.shape[0], PARTS * count)
    row, col = iota(shape, 0), iota(shape, 1)
    source = col & (count - 1)
    wanted = by_index(row >> 3, send.shape[0] // 8, lambda d: plan[d])
    alive = by_index(source, count, alive_of(length, finished))
    chosen = (wanted == source) & ((row & 7) == (col >> 3)) & (alive > 0)
    chosen = jnp.where(chosen, 1.0, 0.0).astype(BF16)
    flat = sub_rows(tokens[...], send.shape[1])
    send[...] = jnp.dot(chosen, flat, preferred_element_type=F32).astype(BF16)
    wait_all(start_all([pltpu.make_async_copy(send, out, sems.at[0])]))


def routing_kernel(plan_hbm, length_hbm, finished_hbm, routes_hbm, score_hbm, tokens_hbm, *rest):
    scatter, gather, flat, plan, length, finished, routes, score, tokens, sems = rest
    pairs = [
        (plan_hbm, plan),
        (length_hbm, length),
        (finished_hbm, finished),
        (routes_hbm, routes),
        (score_hbm, score),
        (tokens_hbm, tokens),
    ]
    wait_all(start_all([pltpu.make_async_copy(*pair, sems.at[n]) for n, pair in enumerate(pairs)]))
    flat[...] = sub_rows(tokens[...], flat.shape[1])
    top, slots = routes.shape
    lanes = scatter.shape[0]
    experts = lanes // 8
    count = slots // 2
    names = jnp.transpose(routes[...].astype(F32))
    scores = jnp.transpose(score[...])
    expert = iota((slots, experts), 1).astype(F32)
    named = jnp.zeros((slots, experts), F32)
    weight = jnp.zeros((slots, experts), F32)
    for k in range(top):
        hit = names[:, k : k + 1] == expert
        named = jnp.where(hit, 1.0, named)
        weight = jnp.where(hit, scores[:, k : k + 1], weight)
    weight = 2.5 * weight / jnp.sum(scores, axis=1, keepdims=True)
    lower = jnp.where(iota((slots, slots), 1) < iota((slots, slots), 0), 1.0, 0.0).astype(BF16)
    position = jnp.dot(lower, named.astype(BF16), preferred_element_type=F32)
    high = weight.astype(BF16).astype(F32)
    low = weight - high
    stacked = jnp.concatenate([named, position, high, low], axis=0).astype(BF16)
    widen = iota((experts, lanes), 0) == (iota((experts, lanes), 1) >> 3)
    wide = jnp.dot(stacked, jnp.where(widen, 1.0, 0.0).astype(BF16), preferred_element_type=F32)
    lane = iota((slots, lanes), 1)
    part = lane & (PARTS - 1)
    place = ((lane >> 2) & 1).astype(F32)
    taken = (wide[:slots] > 0.5) & (wide[slots : 2 * slots] == place)
    taken = jnp.where(taken, 1.0, 0.0)

    row = iota((count, lanes), 0)
    alive = by_index(row, count, alive_of(length, finished))
    moved = jnp.zeros((count, lanes), jnp.int32)
    for d in range(count):
        moved = jnp.where(row == plan[d], 1, moved)
    stays = (alive > 0) & (moved == 0)
    half = part[:count]
    pieces = [jnp.where(stays & (half == q), taken[:count], 0.0) for q in range(PARTS)]
    for i in range(count):
        pieces.append(jnp.where(half == row, taken[count + i : count + i + 1], 0.0))
    used = len(pieces) * count
    pieces.append(jnp.zeros((scatter.shape[1] - used, lanes), F32))
    scatter[...] = jnp.transpose(jnp.concatenate(pieces, axis=0)).astype(BF16)

    pieces = []
    for start in (2 * slots, 3 * slots):
        wanted = wide[start : start + slots] * taken
        pieces += [jnp.where(part == q, wanted, 0.0) for q in range(PARTS)]
    gather[...] = jnp.concatenate(pieces, axis=0).astype(BF16)


def dispatch_kernel(scatter, tokens, arrived, out, block, sems):
    lanes, width = out.shape
    pad = scatter.shape[1] - tokens.shape[0] - arrived.shape[0]
    flat = jnp.concatenate([tokens[...], arrived[...], jnp.zeros((pad, width), BF16)], axis=0)
    copies = []
    for b in range(lanes // 256):
        part = pl.ds(b * 256, 256)
        rows = jnp.dot(scatter[part, :], flat, preferred_element_type=F32)
        block[part, :] = rows.astype(BF16)
        copies += start_all([pltpu.make_async_copy(block.at[part], out.at[part], sems.at[b])])
    wait_all(copies)


def one_hot(hit):
    return jnp.where(hit, 1.0, 0.0).astype(BF16)


def halves(source, target, sems):
    half = source.shape[0] // 2
    parts = [pl.ds(n * half, half) for n in range(2)]
    return [
        pltpu.make_async_copy(source.at[part, :], target.at[part, :], sems.at[n])
        for n, part in enumerate(parts)
    ]


def start_halves(copies):
    for n, copy in enumerate(copies):
        copy.start(priority=n % 2)


def expert_kernel(recv, w_gate, w_up, w_down, out, *scratch):
    gates, ups, downs, rows, results, sent, sems = scratch
    lanes, width = recv.shape
    blocks = lanes // 256
    total = lanes // PARTS
    gate_copies, up_copies, down_copies = [], [], []
    for q in range(PARTS):
        part = slice(q * width, (q + 1) * width)
        gate_copies.append(halves(w_gate.at[0, part, :], gates.at[q], sems.at[0, q]))
        up_copies.append(halves(w_up.at[0, part, :], ups.at[q], sems.at[1, q]))
        down_copies.append(halves(w_down.at[0, :, part], downs.at[q], sems.at[2, q]))
    for q in range(PARTS):
        start_halves(gate_copies[q] + up_copies[q])
    for q in range(PARTS):
        start_halves(down_copies[q])

    one, two = iota((256, 256), 0), iota((256, 256), 1)
    apart = one_hot(((one & 63) * PARTS + (one >> 6)) == two)
    together = one_hot(((two & 63) * PARTS + (two >> 6)) == one)
    used = jnp.zeros((8, total), F32)
    for b in range(blocks):
        part = recv[b * 256 : (b + 1) * 256, :]
        nonzero = jnp.where(part.astype(F32) != 0, 1.0, 0.0).astype(BF16)
        found = lax.dot_general(
            jnp.ones((8, width), BF16),
            nonzero,
            (((1,), (1,)), ((), ())),
            preferred_element_type=F32,
        )
        found = jnp.where(found > 0, 1.0, 0.0).astype(BF16)
        pool = one_hot((iota((256, total), 0) >> 2) + b * 64 == iota((256, total), 1))
        used = used + jnp.dot(found, pool, preferred_element_type=F32)
        got = jnp.dot(apart, part, preferred_element_type=F32).astype(BF16)
        for q in range(PARTS):
            rows[q, b * 64 : (b + 1) * 64, :] = got[q * 64 : (q + 1) * 64, :]
    used = jnp.where(used > 0, 1.0, 0.0)
    before = one_hot(iota((total, total), 0) < iota((total, total), 1))
    place = jnp.dot(used.astype(BF16), before, preferred_element_type=F32)
    count = jnp.sum(used[:1, :]).astype(jnp.int32)

    def body(size):
        pick = (iota((size, total), 0).astype(F32) == place[:1, :]) & (used[:1, :] > 0)
        pick = jnp.where(pick, 1.0, 0.0)
        spread = jnp.transpose(pick).astype(BF16)
        pick = pick.astype(BF16)
        packed = [
            jnp.dot(pick, rows[q], preferred_element_type=F32).astype(BF16) for q in range(PARTS)
        ]
        gate = up = None
        for q in range(PARTS):
            wait_all(gate_copies[q])
            more = jnp.dot(packed[q], gates[q], preferred_element_type=F32)
            gate = more if gate is None else gate + more
            wait_all(up_copies[q])
            more = jnp.dot(packed[q], ups[q], preferred_element_type=F32)
            up = more if up is None else up + more
        hidden = (gate / (1.0 + jnp.exp(-gate)) * up).astype(BF16)
        for q in range(PARTS):
            wait_all(down_copies[q])
            result = jnp.dot(hidden, downs[q], preferred_element_type=F32).astype(BF16)
            result = jnp.dot(spread, result, preferred_element_type=F32).astype(BF16)
            for b in range(blocks):
                results[b, q * 64 : (q + 1) * 64, :] = result[b * 64 : (b + 1) * 64, :]

    small = 160

    @pl.when(count <= small)
    def _():
        body(small)

    @pl.when(count > small)
    def _():
        body(total)

    copies = []
    for b in range(blocks):
        part = pl.ds(b * 256, 256)
        value = jnp.dot(together, results[b], preferred_element_type=F32).astype(BF16)
        sent[part, :] = value
        copies += start_all([pltpu.make_async_copy(sent.at[part], out.at[part], sems.at[0, b, 0])])
    wait_all(copies)


def combine_kernel(gather, recv, out):
    slots = out.shape[0]
    width = recv.shape[1]
    summed = jnp.dot(gather[...], recv[...], preferred_element_type=F32)
    half = summed.shape[0] // 2
    summed = summed[:half] + summed[half:]
    for q in range(PARTS):
        out[:, q * width : (q + 1) * width] = summed[q * slots : (q + 1) * slots].astype(BF16)


def call(kernel, outs, in_specs, cost, scratch=(), limit=32, in_hbm=False):
    shape_of = pltpu.HBM if in_hbm else jax.ShapeDtypeStruct
    shapes = [shape_of(shape, BF16) for shape in outs]
    specs = [HBM if in_hbm else VMEM] * len(outs)
    return pl.pallas_call(
        kernel,
        out_shape=shapes if len(shapes) > 1 else shapes[0],
        in_specs=in_specs,
        out_specs=specs if len(specs) > 1 else specs[0],
        scratch_shapes=list(scratch),
        compiler_params=pltpu.CompilerParams(vmem_limit_bytes=limit * 2**20),
        cost_estimate=pl.CostEstimate(flops=cost[0], bytes_accessed=cost[1], transcendentals=0),
    )


def on_device(
    tokens,
    queries,
    latent_cache,
    new_latent,
    lengths,
    finished,
    migrate,
    routes,
    route_score,
    w_gate,
    w_up,
    w_down,
):
    count, model = tokens.shape
    slots = routes.shape[0]
    replicas = lax.axis_size("replica")
    devices = replicas * lax.axis_size("expert")
    width = model // PARTS
    lanes = devices * CAP * PARTS
    hidden = w_gate.shape[2]
    plan = migrate.reshape(replicas)

    def exchange(values):
        values = values.reshape(devices, 8, width)
        values = lax.all_to_all(values, BOTH, split_axis=0, concat_axis=0, tiled=True)
        return values.reshape(lanes, width)

    def in_hbm(*values):
        return [pltpu.with_memory_space_constraint(value, pltpu.HBM) for value in values]

    integers = [
        pltpu.SMEM((replicas,), jnp.int32),
        pltpu.SMEM((count,), jnp.int32),
        pltpu.SMEM((count,), jnp.int32),
    ]
    send = call(
        pick_kernel,
        [(replicas * 8, width)],
        [HBM] * 4,
        (10**6, 10**5),
        integers
        + [
            pltpu.VMEM((count, model), BF16),
            pltpu.VMEM((replicas * 8, width), BF16),
            pltpu.SemaphoreType.DMA((4,)),
        ],
        in_hbm=True,
    )(*in_hbm(plan, lengths, finished, tokens))
    arrived = lax.all_to_all(
        send.reshape(replicas, 8, width), "replica", split_axis=0, concat_axis=0, tiled=True
    ).reshape(replicas * 8, width)
    scatter, gather, flat = call(
        routing_kernel,
        [(lanes, 128), (2 * PARTS * slots, lanes), (PARTS * count, width)],
        [HBM] * 6,
        (10**7, 10**6),
        integers
        + [
            pltpu.VMEM((routes.shape[1], slots), jnp.int32),
            pltpu.VMEM((routes.shape[1], slots), F32),
            pltpu.VMEM((count, model), BF16),
            pltpu.SemaphoreType.DMA((6,)),
        ],
    )(*in_hbm(plan, lengths, finished, routes.T, route_score.T, tokens))
    outgoing = call(
        dispatch_kernel,
        [(lanes, width)],
        [VMEM] * 3,
        (2 * 10**8, 2 * 10**6),
        [pltpu.VMEM((lanes, width), BF16), pltpu.SemaphoreType.DMA((lanes // 256,))],
        in_hbm=True,
    )(scatter, flat, arrived)
    own_length = jnp.where(finished == 0, lengths, 0)
    held = lax.optimization_barrier((queries, latent_cache, new_latent, plan, outgoing))
    queries, latent_cache, new_latent, plan, outgoing = held
    incoming = exchange(outgoing)

    attended = attend(queries, latent_cache, new_latent, own_length)
    sending = plan >= 0
    moved_out = jnp.any((plan[:, None] == jnp.arange(count)[None, :]), axis=0)
    leave = jnp.where(sending[:, None, None], attended[jnp.maximum(plan, 0)], jnp.zeros((), BF16))
    leave, incoming = lax.optimization_barrier((leave, incoming))
    landed = lax.all_to_all(leave, "replica", split_axis=0, concat_axis=0, tiled=True)
    stay = jnp.where(moved_out[:, None, None], jnp.zeros((), BF16), attended)
    attended_out = jnp.concatenate([stay, landed], axis=0).reshape(slots, HEADS * VDIM)

    results = call(
        expert_kernel,
        [(lanes, width)],
        [VMEM] + [HBM] * 3,
        (6 * devices * CAP * model * hidden, 6 * model * hidden),
        [
            pltpu.VMEM((PARTS, width, hidden), BF16),
            pltpu.VMEM((PARTS, width, hidden), BF16),
            pltpu.VMEM((PARTS, hidden, width), BF16),
            pltpu.VMEM((PARTS, devices * CAP, width), BF16),
            pltpu.VMEM((lanes // 256, 256, width), BF16),
            pltpu.VMEM((lanes, width), BF16),
            pltpu.SemaphoreType.DMA((3, PARTS, 2)),
        ],
        46,
        True,
    )(incoming, *in_hbm(w_gate, w_up, w_down))
    returned = exchange(results)
    expert_out = call(combine_kernel, [(slots, model)], [VMEM] * 2, (2 * 10**8, 2 * 10**6))(
        gather, returned
    )
    return (attended_out, expert_out)


def solution(mesh):
    rows = P(BOTH, None)
    blocks = P(BOTH, None, None)
    flat = P(BOTH)
    return jax.shard_map(
        on_device,
        mesh=mesh,
        in_specs=(rows, rows, blocks, rows, flat, flat, blocks, rows, rows, blocks, blocks, blocks),
        out_specs=(rows, rows),
        check_vma=False,
    )
```

```python
import jax
import jax.numpy as jnp
from jax import lax
from jax.experimental import pallas as pl
from jax.experimental.pallas import tpu as pltpu
from jax.sharding import PartitionSpec as P

HEADS = 64
VDIM = 512
LAT = 576
BOTH = ("replica", "expert")
F32 = jnp.float32
BF16 = jnp.bfloat16

PARTS = 4
CAP = 2
IN_FLIGHT = 3

score_scale = 192.0 ** (-0.5)

VMEM = pl.BlockSpec(memory_space=pltpu.VMEM)
SMEM = pl.BlockSpec(memory_space=pltpu.SMEM)
HBM = pl.BlockSpec(memory_space=pltpu.HBM)


def iota(shape, dim):
    return lax.broadcasted_iota(jnp.int32, shape, dim)


def attend(query_rows, latent_rows, own_latent, live_length):
    row_count = query_rows.shape[0]
    per_head = query_rows.reshape(row_count, HEADS, LAT)
    scores = (
        jnp.einsum("nhl,ntl->nht", per_head, latent_rows, preferred_element_type=F32) * score_scale
    )
    own_score = jnp.einsum("nhl,nl->nh", per_head, own_latent, preferred_element_type=F32)
    own_score = own_score * score_scale
    visible = iota((1, 1, latent_rows.shape[1]), 2) < live_length[:, None, None]
    scores = jnp.where(visible, scores, -jnp.inf)
    largest = jnp.maximum(jnp.max(scores, axis=2), own_score)
    weights = jnp.exp(scores - largest[:, :, None])
    own_weight = jnp.exp(own_score - largest)
    denominator = jnp.sum(weights, axis=2) + own_weight
    context = jnp.einsum(
        "nht,ntv->nhv",
        weights.astype(BF16),
        latent_rows[:, :, :VDIM],
        preferred_element_type=F32,
    )
    own_rounded = lax.optimization_barrier(own_weight.astype(BF16)).astype(F32)
    context = context + own_rounded[:, :, None] * own_latent[:, None, :VDIM].astype(F32)
    normalized = context / denominator[:, :, None] * (live_length > 0).astype(F32)[:, None, None]
    return normalized.astype(BF16)


def by_index(index, count, value_of):
    spread = jnp.zeros(index.shape, jnp.int32)
    for i in range(count):
        spread = jnp.where(index == i, value_of(i), spread)
    return spread


def alive_of(length, finished):
    return lambda s: jnp.where(finished[s] == 0, length[s], 0)


def start_all(copies):
    for copy in copies:
        copy.start()
    return copies


def wait_all(copies):
    for copy in copies:
        copy.wait()


def sub_rows(rows, width):
    pieces = [rows[:, q * width : (q + 1) * width].astype(F32) for q in range(PARTS)]
    return jnp.concatenate(pieces, axis=0).astype(BF16)


def pick_kernel(plan_hbm, length_hbm, finished_hbm, tokens_hbm, out, *scratch):
    plan, length, finished, tokens, send, sems = scratch
    pairs = [
        (plan_hbm, plan),
        (length_hbm, length),
        (finished_hbm, finished),
        (tokens_hbm, tokens),
    ]
    wait_all(start_all([pltpu.make_async_copy(*pair, sems.at[n]) for n, pair in enumerate(pairs)]))
    count = tokens.shape[0]
    shape = (send.shape[0], PARTS * count)
    row, col = iota(shape, 0), iota(shape, 1)
    source = col & (count - 1)
    wanted = by_index(row >> 3, send.shape[0] // 8, lambda d: plan[d])
    alive = by_index(source, count, alive_of(length, finished))
    chosen = (wanted == source) & ((row & 7) == (col >> 3)) & (alive > 0)
    chosen = jnp.where(chosen, 1.0, 0.0).astype(BF16)
    flat = sub_rows(tokens[...], send.shape[1])
    send[...] = jnp.dot(chosen, flat, preferred_element_type=F32).astype(BF16)
    wait_all(start_all([pltpu.make_async_copy(send, out, sems.at[0])]))


def routing_kernel(plan_hbm, length_hbm, finished_hbm, routes_hbm, score_hbm, tokens_hbm, *rest):
    scatter, gather, flat, plan, length, finished, routes, score, tokens, sems = rest
    pairs = [
        (plan_hbm, plan),
        (length_hbm, length),
        (finished_hbm, finished),
        (routes_hbm, routes),
        (score_hbm, score),
        (tokens_hbm, tokens),
    ]
    wait_all(start_all([pltpu.make_async_copy(*pair, sems.at[n]) for n, pair in enumerate(pairs)]))
    flat[...] = sub_rows(tokens[...], flat.shape[1])
    top, slots = routes.shape
    lanes = scatter.shape[0]
    experts = lanes // 8
    count = slots // 2
    names = jnp.transpose(routes[...].astype(F32))
    scores = jnp.transpose(score[...])
    expert = iota((slots, experts), 1).astype(F32)
    named = jnp.zeros((slots, experts), F32)
    weight = jnp.zeros((slots, experts), F32)
    for k in range(top):
        hit = names[:, k : k + 1] == expert
        named = jnp.where(hit, 1.0, named)
        weight = jnp.where(hit, scores[:, k : k + 1], weight)
    weight = 2.5 * weight / jnp.sum(scores, axis=1, keepdims=True)
    lower = jnp.where(iota((slots, slots), 1) < iota((slots, slots), 0), 1.0, 0.0).astype(BF16)
    position = jnp.dot(lower, named.astype(BF16), preferred_element_type=F32)
    high = weight.astype(BF16).astype(F32)
    low = weight - high
    stacked = jnp.concatenate([named, position, high, low], axis=0).astype(BF16)
    widen = iota((experts, lanes), 0) == (iota((experts, lanes), 1) >> 3)
    wide = jnp.dot(stacked, jnp.where(widen, 1.0, 0.0).astype(BF16), preferred_element_type=F32)
    lane = iota((slots, lanes), 1)
    part = lane & (PARTS - 1)
    place = ((lane >> 2) & 1).astype(F32)
    taken = (wide[:slots] > 0.5) & (wide[slots : 2 * slots] == place)
    taken = jnp.where(taken, 1.0, 0.0)

    row = iota((count, lanes), 0)
    alive = by_index(row, count, alive_of(length, finished))
    moved = jnp.zeros((count, lanes), jnp.int32)
    for d in range(count):
        moved = jnp.where(row == plan[d], 1, moved)
    stays = (alive > 0) & (moved == 0)
    half = part[:count]
    pieces = [jnp.where(stays & (half == q), taken[:count], 0.0) for q in range(PARTS)]
    for i in range(count):
        pieces.append(jnp.where(half == row, taken[count + i : count + i + 1], 0.0))
    used = len(pieces) * count
    pieces.append(jnp.zeros((scatter.shape[1] - used, lanes), F32))
    scatter[...] = jnp.transpose(jnp.concatenate(pieces, axis=0)).astype(BF16)

    pieces = []
    for start in (2 * slots, 3 * slots):
        wanted = wide[start : start + slots] * taken
        pieces += [jnp.where(part == q, wanted, 0.0) for q in range(PARTS)]
    gather[...] = jnp.concatenate(pieces, axis=0).astype(BF16)


def dispatch_kernel(scatter, tokens, arrived, out, block, sems):
    lanes, width = out.shape
    pad = scatter.shape[1] - tokens.shape[0] - arrived.shape[0]
    flat = jnp.concatenate([tokens[...], arrived[...], jnp.zeros((pad, width), BF16)], axis=0)
    copies = []
    for b in range(lanes // 256):
        part = pl.ds(b * 256, 256)
        rows = jnp.dot(scatter[part, :], flat, preferred_element_type=F32)
        block[part, :] = rows.astype(BF16)
        copies += start_all([pltpu.make_async_copy(block.at[part], out.at[part], sems.at[b])])
    wait_all(copies)


def one_hot(hit):
    return jnp.where(hit, 1.0, 0.0).astype(BF16)


def expert_kernel(recv, w_gate, w_up, w_down, out, *scratch):
    gates, ups, downs, rows, results, sent, sems = scratch
    lanes, width = recv.shape
    blocks = lanes // 256
    total = lanes // PARTS
    queue = []
    for q in range(PARTS):
        part = pl.ds(q * width, width)
        queue.append(pltpu.make_async_copy(w_gate.at[0, part, :], gates.at[q], sems.at[0, q]))
        queue.append(pltpu.make_async_copy(w_up.at[0, part, :], ups.at[q], sems.at[1, q]))
    for q in range(PARTS):
        part = pl.ds(q * width, width)
        queue.append(pltpu.make_async_copy(w_down.at[0, :, part], downs.at[q], sems.at[2, q]))
    start_all(queue[:IN_FLIGHT])

    def arrive(n):
        queue[n].wait()
        start_all(queue[n + IN_FLIGHT : n + IN_FLIGHT + 1])

    one, two = iota((256, 256), 0), iota((256, 256), 1)
    apart = one_hot(((one & 63) * PARTS + (one >> 6)) == two)
    together = one_hot(((two & 63) * PARTS + (two >> 6)) == one)
    used = jnp.zeros((8, total), F32)
    for b in range(blocks):
        part = recv[b * 256 : (b + 1) * 256, :]
        nonzero = jnp.where(part.astype(F32) != 0, 1.0, 0.0).astype(BF16)
        found = lax.dot_general(
            jnp.ones((8, width), BF16),
            nonzero,
            (((1,), (1,)), ((), ())),
            preferred_element_type=F32,
        )
        found = jnp.where(found > 0, 1.0, 0.0).astype(BF16)
        pool = one_hot((iota((256, total), 0) >> 2) + b * 64 == iota((256, total), 1))
        used = used + jnp.dot(found, pool, preferred_element_type=F32)
        got = jnp.dot(apart, part, preferred_element_type=F32).astype(BF16)
        for q in range(PARTS):
            rows[q, b * 64 : (b + 1) * 64, :] = got[q * 64 : (q + 1) * 64, :]
    used = jnp.where(used > 0, 1.0, 0.0)
    before = one_hot(iota((total, total), 0) < iota((total, total), 1))
    place = jnp.dot(used.astype(BF16), before, preferred_element_type=F32)
    count = jnp.sum(used[:1, :]).astype(jnp.int32)

    def body(size):
        pick = (iota((size, total), 0).astype(F32) == place[:1, :]) & (used[:1, :] > 0)
        pick = jnp.where(pick, 1.0, 0.0)
        spread = jnp.transpose(pick).astype(BF16)
        pick = pick.astype(BF16)
        packed = [
            jnp.dot(pick, rows[q], preferred_element_type=F32).astype(BF16) for q in range(PARTS)
        ]
        gate = up = None
        for q in range(PARTS):
            arrive(2 * q)
            more = jnp.dot(packed[q], gates[q], preferred_element_type=F32)
            gate = more if gate is None else gate + more
            arrive(2 * q + 1)
            more = jnp.dot(packed[q], ups[q], preferred_element_type=F32)
            up = more if up is None else up + more
        hidden = (gate / (1.0 + jnp.exp(-gate)) * up).astype(BF16)
        for q in range(PARTS):
            arrive(2 * PARTS + q)
            result = jnp.dot(hidden, downs[q], preferred_element_type=F32).astype(BF16)
            result = jnp.dot(spread, result, preferred_element_type=F32).astype(BF16)
            for b in range(blocks):
                results[b, q * 64 : (q + 1) * 64, :] = result[b * 64 : (b + 1) * 64, :]

    small = 160

    @pl.when(count <= small)
    def _():
        body(small)

    @pl.when(count > small)
    def _():
        body(total)

    copies = []
    for b in range(blocks):
        part = pl.ds(b * 256, 256)
        value = jnp.dot(together, results[b], preferred_element_type=F32).astype(BF16)
        sent[part, :] = value
        copies += start_all([pltpu.make_async_copy(sent.at[part], out.at[part], sems.at[0, b])])
    wait_all(copies)


def combine_kernel(gather, recv, out):
    slots = out.shape[0]
    width = recv.shape[1]
    summed = jnp.dot(gather[...], recv[...], preferred_element_type=F32)
    half = summed.shape[0] // 2
    summed = summed[:half] + summed[half:]
    for q in range(PARTS):
        out[:, q * width : (q + 1) * width] = summed[q * slots : (q + 1) * slots].astype(BF16)


def call(kernel, outs, in_specs, cost, scratch=(), limit=32, in_hbm=False):
    shape_of = pltpu.HBM if in_hbm else jax.ShapeDtypeStruct
    shapes = [shape_of(shape, BF16) for shape in outs]
    specs = [HBM if in_hbm else VMEM] * len(outs)
    return pl.pallas_call(
        kernel,
        out_shape=shapes if len(shapes) > 1 else shapes[0],
        in_specs=in_specs,
        out_specs=specs if len(specs) > 1 else specs[0],
        scratch_shapes=list(scratch),
        compiler_params=pltpu.CompilerParams(vmem_limit_bytes=limit * 2**20),
        cost_estimate=pl.CostEstimate(flops=cost[0], bytes_accessed=cost[1], transcendentals=0),
    )


def on_device(
    tokens,
    queries,
    latent_cache,
    new_latent,
    lengths,
    finished,
    migrate,
    routes,
    route_score,
    w_gate,
    w_up,
    w_down,
):
    count, model = tokens.shape
    slots = routes.shape[0]
    replicas = lax.axis_size("replica")
    devices = replicas * lax.axis_size("expert")
    width = model // PARTS
    lanes = devices * CAP * PARTS
    hidden = w_gate.shape[2]
    plan = migrate.reshape(replicas)

    def exchange(values):
        values = values.reshape(devices, 8, width)
        values = lax.all_to_all(values, BOTH, split_axis=0, concat_axis=0, tiled=True)
        return values.reshape(lanes, width)

    def in_hbm(*values):
        return [pltpu.with_memory_space_constraint(value, pltpu.HBM) for value in values]

    integers = [
        pltpu.SMEM((replicas,), jnp.int32),
        pltpu.SMEM((count,), jnp.int32),
        pltpu.SMEM((count,), jnp.int32),
    ]
    send = call(
        pick_kernel,
        [(replicas * 8, width)],
        [HBM] * 4,
        (10**6, 10**5),
        integers
        + [
            pltpu.VMEM((count, model), BF16),
            pltpu.VMEM((replicas * 8, width), BF16),
            pltpu.SemaphoreType.DMA((4,)),
        ],
        in_hbm=True,
    )(*in_hbm(plan, lengths, finished, tokens))
    arrived = lax.all_to_all(
        send.reshape(replicas, 8, width), "replica", split_axis=0, concat_axis=0, tiled=True
    ).reshape(replicas * 8, width)
    scatter, gather, flat = call(
        routing_kernel,
        [(lanes, 128), (2 * PARTS * slots, lanes), (PARTS * count, width)],
        [HBM] * 6,
        (10**7, 10**6),
        integers
        + [
            pltpu.VMEM((routes.shape[1], slots), jnp.int32),
            pltpu.VMEM((routes.shape[1], slots), F32),
            pltpu.VMEM((count, model), BF16),
            pltpu.SemaphoreType.DMA((6,)),
        ],
    )(*in_hbm(plan, lengths, finished, routes.T, route_score.T, tokens))
    outgoing = call(
        dispatch_kernel,
        [(lanes, width)],
        [VMEM] * 3,
        (2 * 10**8, 2 * 10**6),
        [pltpu.VMEM((lanes, width), BF16), pltpu.SemaphoreType.DMA((lanes // 256,))],
        in_hbm=True,
    )(scatter, flat, arrived)
    own_length = jnp.where(finished == 0, lengths, 0)
    held = lax.optimization_barrier((queries, latent_cache, new_latent, plan, outgoing))
    queries, latent_cache, new_latent, plan, outgoing = held
    incoming = exchange(outgoing)

    attended = attend(queries, latent_cache, new_latent, own_length)
    sending = plan >= 0
    moved_out = jnp.any((plan[:, None] == jnp.arange(count)[None, :]), axis=0)
    leave = jnp.where(sending[:, None, None], attended[jnp.maximum(plan, 0)], jnp.zeros((), BF16))
    leave, incoming = lax.optimization_barrier((leave, incoming))
    landed = lax.all_to_all(leave, "replica", split_axis=0, concat_axis=0, tiled=True)
    stay = jnp.where(moved_out[:, None, None], jnp.zeros((), BF16), attended)
    attended_out = jnp.concatenate([stay, landed], axis=0).reshape(slots, HEADS * VDIM)

    results = call(
        expert_kernel,
        [(lanes, width)],
        [VMEM] + [HBM] * 3,
        (6 * devices * CAP * model * hidden, 6 * model * hidden),
        [
            pltpu.VMEM((PARTS, width, hidden), BF16),
            pltpu.VMEM((PARTS, width, hidden), BF16),
            pltpu.VMEM((PARTS, hidden, width), BF16),
            pltpu.VMEM((PARTS, devices * CAP, width), BF16),
            pltpu.VMEM((lanes // 256, 256, width), BF16),
            pltpu.VMEM((lanes, width), BF16),
            pltpu.SemaphoreType.DMA((3, 4)),
        ],
        46,
        True,
    )(incoming, *in_hbm(w_gate, w_up, w_down))
    returned = exchange(results)
    expert_out = call(combine_kernel, [(slots, model)], [VMEM] * 2, (2 * 10**8, 2 * 10**6))(
        gather, returned
    )
    return (attended_out, expert_out)


def solution(mesh):
    rows = P(BOTH, None)
    blocks = P(BOTH, None, None)
    flat = P(BOTH)
    return jax.shard_map(
        on_device,
        mesh=mesh,
        in_specs=(rows, rows, blocks, rows, flat, flat, blocks, rows, rows, blocks, blocks, blocks),
        out_specs=(rows, rows),
        check_vma=False,
    )
```

```python
import jax
import jax.numpy as jnp
from jax import lax
from jax.experimental import pallas as pl
from jax.experimental.pallas import tpu as pltpu
from jax.sharding import PartitionSpec as P

HEADS = 64
VDIM = 512
LAT = 576
BOTH = ("replica", "expert")
F32 = jnp.float32
BF16 = jnp.bfloat16

PARTS = 4
CAP = 2

score_scale = 192.0 ** (-0.5)

VMEM = pl.BlockSpec(memory_space=pltpu.VMEM)
SMEM = pl.BlockSpec(memory_space=pltpu.SMEM)
HBM = pl.BlockSpec(memory_space=pltpu.HBM)


def iota(shape, dim):
    return lax.broadcasted_iota(jnp.int32, shape, dim)


def attend(query_rows, latent_rows, own_latent, live_length):
    row_count = query_rows.shape[0]
    per_head = query_rows.reshape(row_count, HEADS, LAT)
    scores = (
        jnp.einsum("nhl,ntl->nht", per_head, latent_rows, preferred_element_type=F32) * score_scale
    )
    own_score = jnp.einsum("nhl,nl->nh", per_head, own_latent, preferred_element_type=F32)
    own_score = own_score * score_scale
    visible = iota((1, 1, latent_rows.shape[1]), 2) < live_length[:, None, None]
    scores = jnp.where(visible, scores, -jnp.inf)
    largest = jnp.maximum(jnp.max(scores, axis=2), own_score)
    weights = jnp.exp(scores - largest[:, :, None])
    own_weight = jnp.exp(own_score - largest)
    denominator = jnp.sum(weights, axis=2) + own_weight
    context = jnp.einsum(
        "nht,ntv->nhv",
        weights.astype(BF16),
        latent_rows[:, :, :VDIM],
        preferred_element_type=F32,
    )
    own_rounded = lax.optimization_barrier(own_weight.astype(BF16)).astype(F32)
    context = context + own_rounded[:, :, None] * own_latent[:, None, :VDIM].astype(F32)
    normalized = context / denominator[:, :, None] * (live_length > 0).astype(F32)[:, None, None]
    return normalized.astype(BF16)


def by_index(index, count, value_of):
    spread = jnp.zeros(index.shape, jnp.int32)
    for i in range(count):
        spread = jnp.where(index == i, value_of(i), spread)
    return spread


def alive_of(length, finished):
    return lambda s: jnp.where(finished[s] == 0, length[s], 0)


def my_replica():
    return lax.axis_index("replica")


def start_all(copies):
    for copy in copies:
        copy.start()
    return copies


def wait_all(copies):
    for copy in copies:
        copy.wait()


def sub_rows(rows, width):
    pieces = [rows[:, q * width : (q + 1) * width].astype(F32) for q in range(PARTS)]
    return jnp.concatenate(pieces, axis=0).astype(BF16)


def pick_kernel(plan_hbm, length_hbm, finished_hbm, tokens_hbm, out, *scratch):
    plan, length, finished, tokens, send, sems = scratch
    pairs = [
        (plan_hbm, plan),
        (length_hbm, length),
        (finished_hbm, finished),
        (tokens_hbm, tokens),
    ]
    wait_all(start_all([pltpu.make_async_copy(*pair, sems.at[n]) for n, pair in enumerate(pairs)]))
    count = tokens.shape[0]
    shape = (send.shape[0], PARTS * count)
    row, col = iota(shape, 0), iota(shape, 1)
    source = col & (count - 1)
    wanted = by_index(row >> 3, send.shape[0] // 8, lambda d: plan[d])
    alive = by_index(source, count, alive_of(length, finished))
    chosen = (wanted == source) & ((row & 7) == (col >> 3)) & (alive > 0)
    chosen = jnp.where(chosen, 1.0, 0.0).astype(BF16)
    flat = sub_rows(tokens[...], send.shape[1])
    send[...] = jnp.dot(chosen, flat, preferred_element_type=F32).astype(BF16)
    wait_all(start_all([pltpu.make_async_copy(send, out, sems.at[0])]))


def routing_kernel(plan_hbm, length_hbm, finished_hbm, routes_hbm, score_hbm, tokens_hbm, *rest):
    scatter, gather, flat, plan, length, finished, routes, score, tokens, sems = rest
    pairs = [
        (plan_hbm, plan),
        (length_hbm, length),
        (finished_hbm, finished),
        (routes_hbm, routes),
        (score_hbm, score),
        (tokens_hbm, tokens),
    ]
    wait_all(start_all([pltpu.make_async_copy(*pair, sems.at[n]) for n, pair in enumerate(pairs)]))
    flat[...] = sub_rows(tokens[...], flat.shape[1])
    top, slots = routes.shape
    lanes = scatter.shape[0]
    experts = lanes // 8
    count = slots // 2
    names = jnp.transpose(routes[...].astype(F32))
    scores = jnp.transpose(score[...])
    expert = iota((slots, experts), 1).astype(F32)
    named = jnp.zeros((slots, experts), F32)
    weight = jnp.zeros((slots, experts), F32)
    for k in range(top):
        hit = names[:, k : k + 1] == expert
        named = jnp.where(hit, 1.0, named)
        weight = jnp.where(hit, scores[:, k : k + 1], weight)
    weight = 2.5 * weight / jnp.sum(scores, axis=1, keepdims=True)
    lower = jnp.where(iota((slots, slots), 1) < iota((slots, slots), 0), 1.0, 0.0).astype(BF16)
    position = jnp.dot(lower, named.astype(BF16), preferred_element_type=F32)
    high = weight.astype(BF16).astype(F32)
    low = weight - high
    stacked = jnp.concatenate([named, position, high, low], axis=0).astype(BF16)
    widen = iota((experts, lanes), 0) == (iota((experts, lanes), 1) >> 3)
    wide = jnp.dot(stacked, jnp.where(widen, 1.0, 0.0).astype(BF16), preferred_element_type=F32)
    lane = iota((slots, lanes), 1)
    part = lane & (PARTS - 1)
    place = ((lane >> 2) & 1).astype(F32)
    taken = (wide[:slots] > 0.5) & (wide[slots : 2 * slots] == place)
    taken = jnp.where(taken, 1.0, 0.0)

    row = iota((count, lanes), 0)
    alive = by_index(row, count, alive_of(length, finished))
    moved = jnp.zeros((count, lanes), jnp.int32)
    for d in range(count):
        moved = jnp.where(row == plan[d], 1, moved)
    stays = (alive > 0) & (moved == 0)
    half = part[:count]
    pieces = [jnp.where(stays & (half == q), taken[:count], 0.0) for q in range(PARTS)]
    for i in range(count):
        pieces.append(jnp.where(half == row, taken[count + i : count + i + 1], 0.0))
    used = len(pieces) * count
    pieces.append(jnp.zeros((scatter.shape[1] - used, lanes), F32))
    scatter[...] = jnp.transpose(jnp.concatenate(pieces, axis=0)).astype(BF16)

    pieces = []
    for start in (2 * slots, 3 * slots):
        wanted = wide[start : start + slots] * taken
        pieces += [jnp.where(part == q, wanted, 0.0) for q in range(PARTS)]
    gather[...] = jnp.concatenate(pieces, axis=0).astype(BF16)


def dispatch_kernel(scatter, tokens, arrived, out, block, sems):
    lanes, width = out.shape
    pad = scatter.shape[1] - tokens.shape[0] - arrived.shape[0]
    flat = jnp.concatenate([tokens[...], arrived[...], jnp.zeros((pad, width), BF16)], axis=0)
    copies = []
    for b in range(lanes // 256):
        part = pl.ds(b * 256, 256)
        rows = jnp.dot(scatter[part, :], flat, preferred_element_type=F32)
        block[part, :] = rows.astype(BF16)
        copies += start_all([pltpu.make_async_copy(block.at[part], out.at[part], sems.at[b])])
    wait_all(copies)


def one_hot(hit):
    return jnp.where(hit, 1.0, 0.0).astype(BF16)


def expert_kernel(recv, w_gate, w_up, w_down, out, *scratch):
    gates, ups, downs, rows, results, sent, sems = scratch
    lanes, width = recv.shape
    blocks = lanes // 256
    total = lanes // PARTS
    gate_copies, up_copies, down_copies = [], [], []
    for q in range(PARTS):
        part = pl.ds(q * width, width)
        gate_copies.append(pltpu.make_async_copy(w_gate.at[0, part, :], gates.at[q], sems.at[0, q]))
        up_copies.append(pltpu.make_async_copy(w_up.at[0, part, :], ups.at[q], sems.at[1, q]))
        down_copies.append(
            pltpu.make_async_copy(w_down.at[0, :, part], downs.at[q], sems.at[2, q])
        )
        start_all([gate_copies[q], up_copies[q]])
    start_all(down_copies)

    one, two = iota((256, 256), 0), iota((256, 256), 1)
    apart = one_hot(((one & 63) * PARTS + (one >> 6)) == two)
    together = one_hot(((two & 63) * PARTS + (two >> 6)) == one)
    used = jnp.zeros((8, total), F32)
    for b in range(blocks):
        part = recv[b * 256 : (b + 1) * 256, :]
        nonzero = jnp.where(part.astype(F32) != 0, 1.0, 0.0).astype(BF16)
        found = lax.dot_general(
            jnp.ones((8, width), BF16),
            nonzero,
            (((1,), (1,)), ((), ())),
            preferred_element_type=F32,
        )
        found = jnp.where(found > 0, 1.0, 0.0).astype(BF16)
        pool = one_hot((iota((256, total), 0) >> 2) + b * 64 == iota((256, total), 1))
        used = used + jnp.dot(found, pool, preferred_element_type=F32)
        got = jnp.dot(apart, part, preferred_element_type=F32).astype(BF16)
        for q in range(PARTS):
            rows[q, b * 64 : (b + 1) * 64, :] = got[q * 64 : (q + 1) * 64, :]
    used = jnp.where(used > 0, 1.0, 0.0)
    before = one_hot(iota((total, total), 0) < iota((total, total), 1))
    place = jnp.dot(used.astype(BF16), before, preferred_element_type=F32)
    count = jnp.sum(used[:1, :]).astype(jnp.int32)

    def body(size):
        pick = (iota((size, total), 0).astype(F32) == place[:1, :]) & (used[:1, :] > 0)
        pick = jnp.where(pick, 1.0, 0.0)
        spread = jnp.transpose(pick).astype(BF16)
        pick = pick.astype(BF16)
        packed = [
            jnp.dot(pick, rows[q], preferred_element_type=F32).astype(BF16) for q in range(PARTS)
        ]
        gate = up = None
        for q in range(PARTS):
            gate_copies[q].wait()
            more = jnp.dot(packed[q], gates[q], preferred_element_type=F32)
            gate = more if gate is None else gate + more
            up_copies[q].wait()
            more = jnp.dot(packed[q], ups[q], preferred_element_type=F32)
            up = more if up is None else up + more
        hidden = (gate / (1.0 + jnp.exp(-gate)) * up).astype(BF16)
        for q in range(PARTS):
            down_copies[q].wait()
            result = jnp.dot(hidden, downs[q], preferred_element_type=F32).astype(BF16)
            result = jnp.dot(spread, result, preferred_element_type=F32).astype(BF16)
            for b in range(blocks):
                results[b, q * 64 : (q + 1) * 64, :] = result[b * 64 : (b + 1) * 64, :]

    small = 160

    @pl.when(count <= small)
    def _():
        body(small)

    @pl.when(count > small)
    def _():
        body(total)

    copies = []
    for b in range(blocks):
        part = pl.ds(b * 256, 256)
        value = jnp.dot(together, results[b], preferred_element_type=F32).astype(BF16)
        sent[part, :] = value
        copies += start_all([pltpu.make_async_copy(sent.at[part], out.at[part], sems.at[0, b])])
    wait_all(copies)


def leave_kernel(plan, attended, *outs):
    for k, out in enumerate(outs, 1):
        row = plan[my_replica() ^ k]
        kept = jnp.where(row >= 0, 1.0, 0.0)
        out[...] = (attended[jnp.maximum(row, 0)].astype(F32) * kept).astype(BF16)


def land_kernel(plan, attended, *rest):
    arrived, out = rest[:-1], rest[-1]
    count = attended.shape[0]
    for s in range(count):
        moved = jnp.int32(0)
        for d in range(count):
            moved = jnp.where(plan[d] == s, 1, moved)
        kept = jnp.where(moved == 0, 1.0, 0.0)
        out[s] = (attended[s].astype(F32) * kept).astype(BF16)
    out[count + my_replica()] = jnp.zeros(out.shape[1:], BF16)
    for k, value in enumerate(arrived, 1):
        out[count + (my_replica() ^ k)] = value[...]


def combine_kernel(gather, recv, out):
    slots = out.shape[0]
    width = recv.shape[1]
    summed = jnp.dot(gather[...], recv[...], preferred_element_type=F32)
    half = summed.shape[0] // 2
    summed = summed[:half] + summed[half:]
    for q in range(PARTS):
        out[:, q * width : (q + 1) * width] = summed[q * slots : (q + 1) * slots].astype(BF16)


def call(kernel, outs, in_specs, cost, scratch=(), limit=32, in_hbm=False):
    shape_of = pltpu.HBM if in_hbm else jax.ShapeDtypeStruct
    shapes = [shape_of(shape, BF16) for shape in outs]
    specs = [HBM if in_hbm else VMEM] * len(outs)
    return pl.pallas_call(
        kernel,
        out_shape=shapes if len(shapes) > 1 else shapes[0],
        in_specs=in_specs,
        out_specs=specs if len(specs) > 1 else specs[0],
        scratch_shapes=list(scratch),
        compiler_params=pltpu.CompilerParams(vmem_limit_bytes=limit * 2**20),
        cost_estimate=pl.CostEstimate(flops=cost[0], bytes_accessed=cost[1], transcendentals=0),
    )


def on_device(
    tokens,
    queries,
    latent_cache,
    new_latent,
    lengths,
    finished,
    migrate,
    routes,
    route_score,
    w_gate,
    w_up,
    w_down,
):
    count, model = tokens.shape
    slots = routes.shape[0]
    replicas = lax.axis_size("replica")
    devices = replicas * lax.axis_size("expert")
    width = model // PARTS
    lanes = devices * CAP * PARTS
    hidden = w_gate.shape[2]
    plan = migrate.reshape(replicas)

    def exchange(values):
        values = values.reshape(devices, 8, width)
        values = lax.all_to_all(values, BOTH, split_axis=0, concat_axis=0, tiled=True)
        return values.reshape(lanes, width)

    def in_hbm(*values):
        return [pltpu.with_memory_space_constraint(value, pltpu.HBM) for value in values]

    integers = [
        pltpu.SMEM((replicas,), jnp.int32),
        pltpu.SMEM((count,), jnp.int32),
        pltpu.SMEM((count,), jnp.int32),
    ]
    send = call(
        pick_kernel,
        [(replicas * 8, width)],
        [HBM] * 4,
        (10**6, 10**5),
        integers
        + [
            pltpu.VMEM((count, model), BF16),
            pltpu.VMEM((replicas * 8, width), BF16),
            pltpu.SemaphoreType.DMA((4,)),
        ],
        in_hbm=True,
    )(*in_hbm(plan, lengths, finished, tokens))
    arrived = lax.all_to_all(
        send.reshape(replicas, 8, width), "replica", split_axis=0, concat_axis=0, tiled=True
    ).reshape(replicas * 8, width)
    scatter, gather, flat = call(
        routing_kernel,
        [(lanes, 128), (2 * PARTS * slots, lanes), (PARTS * count, width)],
        [HBM] * 6,
        (10**7, 10**6),
        integers
        + [
            pltpu.VMEM((routes.shape[1], slots), jnp.int32),
            pltpu.VMEM((routes.shape[1], slots), F32),
            pltpu.VMEM((count, model), BF16),
            pltpu.SemaphoreType.DMA((6,)),
        ],
    )(*in_hbm(plan, lengths, finished, routes.T, route_score.T, tokens))
    outgoing = call(
        dispatch_kernel,
        [(lanes, width)],
        [VMEM] * 3,
        (2 * 10**8, 2 * 10**6),
        [pltpu.VMEM((lanes, width), BF16), pltpu.SemaphoreType.DMA((lanes // 256,))],
        in_hbm=True,
    )(scatter, flat, arrived)
    own_length = jnp.where(finished == 0, lengths, 0)
    held = lax.optimization_barrier((queries, new_latent, outgoing))
    queries, new_latent, outgoing = held
    incoming = exchange(outgoing)

    attended = attend(queries, latent_cache, new_latent, own_length)
    leave = call(
        leave_kernel,
        [(HEADS, VDIM)] * (replicas - 1),
        [SMEM, VMEM],
        (10**6, 10**6),
    )(plan, attended)
    landed = []
    for k, value in enumerate(leave, 1):
        landed.append(lax.ppermute(value, "replica", [(i, i ^ k) for i in range(replicas)]))
    *landed, incoming = lax.optimization_barrier((*landed, incoming))
    attended_out = call(
        land_kernel,
        [(slots, HEADS, VDIM)],
        [SMEM] + [VMEM] * replicas,
        (10**6, 4 * 10**6),
    )(plan, attended, *landed).reshape(slots, HEADS * VDIM)

    results = call(
        expert_kernel,
        [(lanes, width)],
        [VMEM] + [HBM] * 3,
        (6 * devices * CAP * model * hidden, 6 * model * hidden),
        [
            pltpu.VMEM((PARTS, width, hidden), BF16),
            pltpu.VMEM((PARTS, width, hidden), BF16),
            pltpu.VMEM((PARTS, hidden, width), BF16),
            pltpu.VMEM((PARTS, devices * CAP, width), BF16),
            pltpu.VMEM((lanes // 256, 256, width), BF16),
            pltpu.VMEM((lanes, width), BF16),
            pltpu.SemaphoreType.DMA((3, 4)),
        ],
        46,
        True,
    )(incoming, *in_hbm(w_gate, w_up, w_down))
    returned = exchange(results)
    expert_out = call(combine_kernel, [(slots, model)], [VMEM] * 2, (2 * 10**8, 2 * 10**6))(
        gather, returned
    )
    return (attended_out, expert_out)


def solution(mesh):
    rows = P(BOTH, None)
    blocks = P(BOTH, None, None)
    flat = P(BOTH)
    return jax.shard_map(
        on_device,
        mesh=mesh,
        in_specs=(rows, rows, blocks, rows, flat, flat, blocks, rows, rows, blocks, blocks, blocks),
        out_specs=(rows, rows),
        check_vma=False,
    )
```

```python
import jax
import jax.numpy as jnp
from jax import lax
from jax.experimental import pallas as pl
from jax.experimental.pallas import tpu as pltpu
from jax.sharding import PartitionSpec as P

HEADS = 64
VDIM = 512
LAT = 576
BOTH = ("replica", "expert")
F32 = jnp.float32
BF16 = jnp.bfloat16

PARTS = 4
CAP = 2

score_scale = 192.0 ** (-0.5)

VMEM = pl.BlockSpec(memory_space=pltpu.VMEM)
SMEM = pl.BlockSpec(memory_space=pltpu.SMEM)
HBM = pl.BlockSpec(memory_space=pltpu.HBM)


def iota(shape, dim):
    return lax.broadcasted_iota(jnp.int32, shape, dim)


def attend(query_rows, latent_rows, own_latent, live_length):
    row_count = query_rows.shape[0]
    per_head = query_rows.reshape(row_count, HEADS, LAT)
    scores = (
        jnp.einsum("nhl,ntl->nht", per_head, latent_rows, preferred_element_type=F32) * score_scale
    )
    own_score = jnp.einsum("nhl,nl->nh", per_head, own_latent, preferred_element_type=F32)
    own_score = own_score * score_scale
    visible = iota((1, 1, latent_rows.shape[1]), 2) < live_length[:, None, None]
    scores = jnp.where(visible, scores, -jnp.inf)
    largest = jnp.maximum(jnp.max(scores, axis=2), own_score)
    weights = jnp.exp(scores - largest[:, :, None])
    own_weight = jnp.exp(own_score - largest)
    denominator = jnp.sum(weights, axis=2) + own_weight
    context = jnp.einsum(
        "nht,ntv->nhv",
        weights.astype(BF16),
        latent_rows[:, :, :VDIM],
        preferred_element_type=F32,
    )
    own_rounded = lax.optimization_barrier(own_weight.astype(BF16)).astype(F32)
    context = context + own_rounded[:, :, None] * own_latent[:, None, :VDIM].astype(F32)
    normalized = context / denominator[:, :, None] * (live_length > 0).astype(F32)[:, None, None]
    return normalized.astype(BF16)


def by_index(index, count, value_of):
    spread = jnp.zeros(index.shape, jnp.int32)
    for i in range(count):
        spread = jnp.where(index == i, value_of(i), spread)
    return spread


def alive_of(length, finished):
    return lambda s: jnp.where(finished[s] == 0, length[s], 0)


def my_replica():
    return lax.axis_index("replica")


def start_all(copies):
    for copy in copies:
        copy.start()
    return copies


def wait_all(copies):
    for copy in copies:
        copy.wait()


def sub_rows(rows, width):
    pieces = [rows[:, q * width : (q + 1) * width].astype(F32) for q in range(PARTS)]
    return jnp.concatenate(pieces, axis=0).astype(BF16)


def pick_kernel(plan_hbm, length_hbm, finished_hbm, tokens_hbm, out, *scratch):
    plan, length, finished, tokens, send, sems = scratch
    pairs = [
        (plan_hbm, plan),
        (length_hbm, length),
        (finished_hbm, finished),
        (tokens_hbm, tokens),
    ]
    wait_all(start_all([pltpu.make_async_copy(*pair, sems.at[n]) for n, pair in enumerate(pairs)]))
    count = tokens.shape[0]
    shape = (send.shape[0], PARTS * count)
    row, col = iota(shape, 0), iota(shape, 1)
    source = col & (count - 1)
    wanted = by_index(row >> 3, send.shape[0] // 8, lambda d: plan[d])
    alive = by_index(source, count, alive_of(length, finished))
    chosen = (wanted == source) & ((row & 7) == (col >> 3)) & (alive > 0)
    chosen = jnp.where(chosen, 1.0, 0.0).astype(BF16)
    flat = sub_rows(tokens[...], send.shape[1])
    send[...] = jnp.dot(chosen, flat, preferred_element_type=F32).astype(BF16)
    wait_all(start_all([pltpu.make_async_copy(send, out, sems.at[0])]))


def routing_kernel(plan_hbm, length_hbm, finished_hbm, routes_hbm, score_hbm, tokens_hbm, *rest):
    scatter, gather, flat, plan, length, finished, routes, score, tokens, sems = rest
    pairs = [
        (plan_hbm, plan),
        (length_hbm, length),
        (finished_hbm, finished),
        (routes_hbm, routes),
        (score_hbm, score),
        (tokens_hbm, tokens),
    ]
    wait_all(start_all([pltpu.make_async_copy(*pair, sems.at[n]) for n, pair in enumerate(pairs)]))
    flat[...] = sub_rows(tokens[...], flat.shape[1])
    top, slots = routes.shape
    lanes = scatter.shape[0]
    experts = lanes // 8
    count = slots // 2
    names = jnp.transpose(routes[...].astype(F32))
    scores = jnp.transpose(score[...])
    expert = iota((slots, experts), 1).astype(F32)
    named = jnp.zeros((slots, experts), F32)
    weight = jnp.zeros((slots, experts), F32)
    for k in range(top):
        hit = names[:, k : k + 1] == expert
        named = jnp.where(hit, 1.0, named)
        weight = jnp.where(hit, scores[:, k : k + 1], weight)
    weight = 2.5 * weight / jnp.sum(scores, axis=1, keepdims=True)
    lower = jnp.where(iota((slots, slots), 1) < iota((slots, slots), 0), 1.0, 0.0).astype(BF16)
    position = jnp.dot(lower, named.astype(BF16), preferred_element_type=F32)
    high = weight.astype(BF16).astype(F32)
    low = weight - high
    stacked = jnp.concatenate([named, position, high, low], axis=0).astype(BF16)
    widen = iota((experts, lanes), 0) == (iota((experts, lanes), 1) >> 3)
    wide = jnp.dot(stacked, jnp.where(widen, 1.0, 0.0).astype(BF16), preferred_element_type=F32)
    lane = iota((slots, lanes), 1)
    part = lane & (PARTS - 1)
    place = ((lane >> 2) & 1).astype(F32)
    taken = (wide[:slots] > 0.5) & (wide[slots : 2 * slots] == place)
    taken = jnp.where(taken, 1.0, 0.0)

    row = iota((count, lanes), 0)
    alive = by_index(row, count, alive_of(length, finished))
    moved = jnp.zeros((count, lanes), jnp.int32)
    for d in range(count):
        moved = jnp.where(row == plan[d], 1, moved)
    stays = (alive > 0) & (moved == 0)
    half = part[:count]
    pieces = [jnp.where(stays & (half == q), taken[:count], 0.0) for q in range(PARTS)]
    for i in range(count):
        pieces.append(jnp.where(half == row, taken[count + i : count + i + 1], 0.0))
    used = len(pieces) * count
    pieces.append(jnp.zeros((scatter.shape[1] - used, lanes), F32))
    scatter[...] = jnp.transpose(jnp.concatenate(pieces, axis=0)).astype(BF16)

    pieces = []
    for start in (2 * slots, 3 * slots):
        wanted = wide[start : start + slots] * taken
        pieces += [jnp.where(part == q, wanted, 0.0) for q in range(PARTS)]
    gather[...] = jnp.concatenate(pieces, axis=0).astype(BF16)


def dispatch_kernel(scatter, tokens, arrived, out, block, sems):
    lanes, width = out.shape
    pad = scatter.shape[1] - tokens.shape[0] - arrived.shape[0]
    flat = jnp.concatenate([tokens[...], arrived[...], jnp.zeros((pad, width), BF16)], axis=0)
    copies = []
    for b in range(lanes // 256):
        part = pl.ds(b * 256, 256)
        rows = jnp.dot(scatter[part, :], flat, preferred_element_type=F32)
        block[part, :] = rows.astype(BF16)
        copies += start_all([pltpu.make_async_copy(block.at[part], out.at[part], sems.at[b])])
    wait_all(copies)


def one_hot(hit):
    return jnp.where(hit, 1.0, 0.0).astype(BF16)


def expert_kernel(recv, w_gate, w_up, w_down, out, *scratch):
    gates, ups, downs, rows, results, sent, sems = scratch
    lanes, width = recv.shape
    blocks = lanes // 256
    total = lanes // PARTS
    gate_copies, up_copies, down_copies = [], [], []
    for q in range(PARTS):
        part = pl.ds(q * width, width)
        gate_copies.append(pltpu.make_async_copy(w_gate.at[0, part, :], gates.at[q], sems.at[0, q]))
        up_copies.append(pltpu.make_async_copy(w_up.at[0, part, :], ups.at[q], sems.at[1, q]))
        down_copies.append(
            pltpu.make_async_copy(w_down.at[0, :, part], downs.at[q], sems.at[2, q])
        )
        start_all([gate_copies[q], up_copies[q]])
    start_all(down_copies)

    one, two = iota((256, 256), 0), iota((256, 256), 1)
    apart = one_hot(((one & 63) * PARTS + (one >> 6)) == two)
    together = one_hot(((two & 63) * PARTS + (two >> 6)) == one)
    used = jnp.zeros((8, total), F32)
    for b in range(blocks):
        part = recv[b * 256 : (b + 1) * 256, :]
        nonzero = jnp.where(part.astype(F32) != 0, 1.0, 0.0).astype(BF16)
        found = lax.dot_general(
            jnp.ones((8, width), BF16),
            nonzero,
            (((1,), (1,)), ((), ())),
            preferred_element_type=F32,
        )
        found = jnp.where(found > 0, 1.0, 0.0).astype(BF16)
        pool = one_hot((iota((256, total), 0) >> 2) + b * 64 == iota((256, total), 1))
        used = used + jnp.dot(found, pool, preferred_element_type=F32)
        got = jnp.dot(apart, part, preferred_element_type=F32).astype(BF16)
        for q in range(PARTS):
            rows[q, b * 64 : (b + 1) * 64, :] = got[q * 64 : (q + 1) * 64, :]
    used = jnp.where(used > 0, 1.0, 0.0)
    before = one_hot(iota((total, total), 0) < iota((total, total), 1))
    place = jnp.dot(used.astype(BF16), before, preferred_element_type=F32)
    count = jnp.sum(used[:1, :]).astype(jnp.int32)

    def body(size):
        pick = (iota((size, total), 0).astype(F32) == place[:1, :]) & (used[:1, :] > 0)
        pick = jnp.where(pick, 1.0, 0.0)
        spread = jnp.transpose(pick).astype(BF16)
        pick = pick.astype(BF16)
        packed = [
            jnp.dot(pick, rows[q], preferred_element_type=F32).astype(BF16) for q in range(PARTS)
        ]
        gate = up = None
        for q in range(PARTS):
            gate_copies[q].wait()
            more = jnp.dot(packed[q], gates[q], preferred_element_type=F32)
            gate = more if gate is None else gate + more
            up_copies[q].wait()
            more = jnp.dot(packed[q], ups[q], preferred_element_type=F32)
            up = more if up is None else up + more
        hidden = (gate / (1.0 + jnp.exp(-gate)) * up).astype(BF16)
        for q in range(PARTS):
            down_copies[q].wait()
            result = jnp.dot(hidden, downs[q], preferred_element_type=F32).astype(BF16)
            result = jnp.dot(spread, result, preferred_element_type=F32).astype(BF16)
            for b in range(blocks):
                results[b, q * 64 : (q + 1) * 64, :] = result[b * 64 : (b + 1) * 64, :]

    small = 160

    @pl.when(count <= small)
    def _():
        body(small)

    @pl.when(count > small)
    def _():
        body(total)

    copies = []
    for b in range(blocks):
        part = pl.ds(b * 256, 256)
        value = jnp.dot(together, results[b], preferred_element_type=F32).astype(BF16)
        sent[part, :] = value
        copies += start_all([pltpu.make_async_copy(sent.at[part], out.at[part], sems.at[0, b])])
    wait_all(copies)


def leave_kernel(plan, attended, own, beside):
    for n in range(own.shape[0]):
        for core, out in enumerate((own, beside)):
            row = plan[my_replica() ^ (2 * n + core)]
            kept = jnp.where(row >= 0, 1.0, 0.0)
            out[n] = (attended[jnp.maximum(row, 0)].astype(F32) * kept).astype(BF16)


def pair_kernel(own, handed, *outs):
    for n, out in enumerate(outs, 1):
        out[0] = own[n]
        out[1] = handed[n]


def land_kernel(plan, attended, handed, *rest):
    arrived, out = rest[:-2], rest[-1]
    count = attended.shape[0]
    me = my_replica()
    for s in range(count):
        moved = jnp.int32(0)
        for d in range(count):
            moved = jnp.where(plan[d] == s, 1, moved)
        kept = jnp.where(moved == 0, 1.0, 0.0)
        out[s] = (attended[s].astype(F32) * kept).astype(BF16)
    out[count + me] = jnp.zeros(out.shape[1:], BF16)
    out[count + (me ^ 1)] = handed[0]
    for n, rows in enumerate(arrived, 1):
        for core in range(2):
            out[count + (me ^ (2 * n + core))] = rows[core]


def combine_kernel(gather, recv, out):
    slots = out.shape[0]
    width = recv.shape[1]
    summed = jnp.dot(gather[...], recv[...], preferred_element_type=F32)
    half = summed.shape[0] // 2
    summed = summed[:half] + summed[half:]
    for q in range(PARTS):
        out[:, q * width : (q + 1) * width] = summed[q * slots : (q + 1) * slots].astype(BF16)


def call(kernel, outs, in_specs, cost, scratch=(), limit=32, in_hbm=False):
    shape_of = pltpu.HBM if in_hbm else jax.ShapeDtypeStruct
    shapes = [shape_of(shape, BF16) for shape in outs]
    specs = [HBM if in_hbm else VMEM] * len(outs)
    return pl.pallas_call(
        kernel,
        out_shape=shapes if len(shapes) > 1 else shapes[0],
        in_specs=in_specs,
        out_specs=specs if len(specs) > 1 else specs[0],
        scratch_shapes=list(scratch),
        compiler_params=pltpu.CompilerParams(vmem_limit_bytes=limit * 2**20),
        cost_estimate=pl.CostEstimate(flops=cost[0], bytes_accessed=cost[1], transcendentals=0),
    )


def on_device(
    tokens,
    queries,
    latent_cache,
    new_latent,
    lengths,
    finished,
    migrate,
    routes,
    route_score,
    w_gate,
    w_up,
    w_down,
):
    count, model = tokens.shape
    slots = routes.shape[0]
    replicas = lax.axis_size("replica")
    devices = replicas * lax.axis_size("expert")
    width = model // PARTS
    lanes = devices * CAP * PARTS
    hidden = w_gate.shape[2]
    plan = migrate.reshape(replicas)

    def exchange(values):
        values = values.reshape(devices, 8, width)
        values = lax.all_to_all(values, BOTH, split_axis=0, concat_axis=0, tiled=True)
        return values.reshape(lanes, width)

    def in_hbm(*values):
        return [pltpu.with_memory_space_constraint(value, pltpu.HBM) for value in values]

    integers = [
        pltpu.SMEM((replicas,), jnp.int32),
        pltpu.SMEM((count,), jnp.int32),
        pltpu.SMEM((count,), jnp.int32),
    ]
    send = call(
        pick_kernel,
        [(replicas * 8, width)],
        [HBM] * 4,
        (10**6, 10**5),
        integers
        + [
            pltpu.VMEM((count, model), BF16),
            pltpu.VMEM((replicas * 8, width), BF16),
            pltpu.SemaphoreType.DMA((4,)),
        ],
        in_hbm=True,
    )(*in_hbm(plan, lengths, finished, tokens))
    arrived = lax.all_to_all(
        send.reshape(replicas, 8, width), "replica", split_axis=0, concat_axis=0, tiled=True
    ).reshape(replicas * 8, width)
    scatter, gather, flat = call(
        routing_kernel,
        [(lanes, 128), (2 * PARTS * slots, lanes), (PARTS * count, width)],
        [HBM] * 6,
        (10**7, 10**6),
        integers
        + [
            pltpu.VMEM((routes.shape[1], slots), jnp.int32),
            pltpu.VMEM((routes.shape[1], slots), F32),
            pltpu.VMEM((count, model), BF16),
            pltpu.SemaphoreType.DMA((6,)),
        ],
    )(*in_hbm(plan, lengths, finished, routes.T, route_score.T, tokens))
    outgoing = call(
        dispatch_kernel,
        [(lanes, width)],
        [VMEM] * 3,
        (2 * 10**8, 2 * 10**6),
        [pltpu.VMEM((lanes, width), BF16), pltpu.SemaphoreType.DMA((lanes // 256,))],
        in_hbm=True,
    )(scatter, flat, arrived)
    own_length = jnp.where(finished == 0, lengths, 0)
    held = lax.optimization_barrier((queries, new_latent, outgoing))
    queries, new_latent, outgoing = held
    incoming = exchange(outgoing)

    attended = attend(queries, latent_cache, new_latent, own_length)
    def swap(values, k):
        return lax.ppermute(values, "replica", [(i, i ^ k) for i in range(replicas)])

    chips = replicas // 2
    own, beside = call(
        leave_kernel,
        [(chips, HEADS, VDIM)] * 2,
        [SMEM, VMEM],
        (10**6, 10**6),
    )(plan, attended)
    handed = swap(beside, 1)
    pairs = call(
        pair_kernel,
        [(2, HEADS, VDIM)] * (chips - 1),
        [VMEM] * 2,
        (10**6, 10**6),
    )(own, handed)
    landed = [swap(pair, 2 * n) for n, pair in enumerate(pairs, 1)]
    *landed, incoming = lax.optimization_barrier((*landed, incoming))
    results = call(
        expert_kernel,
        [(lanes, width)],
        [VMEM] + [HBM] * 3,
        (6 * devices * CAP * model * hidden, 6 * model * hidden),
        [
            pltpu.VMEM((PARTS, width, hidden), BF16),
            pltpu.VMEM((PARTS, width, hidden), BF16),
            pltpu.VMEM((PARTS, hidden, width), BF16),
            pltpu.VMEM((PARTS, devices * CAP, width), BF16),
            pltpu.VMEM((lanes // 256, 256, width), BF16),
            pltpu.VMEM((lanes, width), BF16),
            pltpu.SemaphoreType.DMA((3, 4)),
        ],
        46,
        True,
    )(incoming, *in_hbm(w_gate, w_up, w_down))
    returned = exchange(results)
    attended_out = call(
        land_kernel,
        [(slots, HEADS, VDIM)],
        [SMEM] + [VMEM] * (1 + chips) + [HBM],
        (10**6, 4 * 10**6),
    )(plan, attended, handed, *landed, *in_hbm(results)).reshape(slots, HEADS * VDIM)
    expert_out = call(combine_kernel, [(slots, model)], [VMEM] * 2, (2 * 10**8, 2 * 10**6))(
        gather, returned
    )
    return (attended_out, expert_out)


def solution(mesh):
    rows = P(BOTH, None)
    blocks = P(BOTH, None, None)
    flat = P(BOTH)
    return jax.shard_map(
        on_device,
        mesh=mesh,
        in_specs=(rows, rows, blocks, rows, flat, flat, blocks, rows, rows, blocks, blocks, blocks),
        out_specs=(rows, rows),
        check_vma=False,
    )
```

```python
import jax
import jax.numpy as jnp
from jax import lax
from jax.experimental import pallas as pl
from jax.experimental.pallas import tpu as pltpu
from jax.sharding import PartitionSpec as P

HEADS = 64
VDIM = 512
LAT = 576
BOTH = ("replica", "expert")
F32 = jnp.float32
BF16 = jnp.bfloat16

PARTS = 4
CAP = 2

score_scale = 192.0 ** (-0.5)

VMEM = pl.BlockSpec(memory_space=pltpu.VMEM)
SMEM = pl.BlockSpec(memory_space=pltpu.SMEM)
HBM = pl.BlockSpec(memory_space=pltpu.HBM)


def iota(shape, dim):
    return lax.broadcasted_iota(jnp.int32, shape, dim)


def attend(query_rows, latent_rows, own_latent, live_length):
    row_count = query_rows.shape[0]
    per_head = query_rows.reshape(row_count, HEADS, LAT)
    scores = (
        jnp.einsum("nhl,ntl->nht", per_head, latent_rows, preferred_element_type=F32) * score_scale
    )
    own_score = jnp.einsum("nhl,nl->nh", per_head, own_latent, preferred_element_type=F32)
    own_score = own_score * score_scale
    visible = iota((1, 1, latent_rows.shape[1]), 2) < live_length[:, None, None]
    scores = jnp.where(visible, scores, -jnp.inf)
    largest = jnp.maximum(jnp.max(scores, axis=2), own_score)
    weights = jnp.exp(scores - largest[:, :, None])
    own_weight = jnp.exp(own_score - largest)
    denominator = jnp.sum(weights, axis=2) + own_weight
    context = jnp.einsum(
        "nht,ntv->nhv",
        weights.astype(BF16),
        latent_rows[:, :, :VDIM],
        preferred_element_type=F32,
    )
    own_rounded = lax.optimization_barrier(own_weight.astype(BF16)).astype(F32)
    context = context + own_rounded[:, :, None] * own_latent[:, None, :VDIM].astype(F32)
    normalized = context / denominator[:, :, None] * (live_length > 0).astype(F32)[:, None, None]
    return normalized.astype(BF16)


def by_index(index, count, value_of):
    spread = jnp.zeros(index.shape, jnp.int32)
    for i in range(count):
        spread = jnp.where(index == i, value_of(i), spread)
    return spread


def alive_of(length, finished):
    return lambda s: jnp.where(finished[s] == 0, length[s], 0)


def my_replica():
    return lax.axis_index("replica")


def start_all(copies):
    for copy in copies:
        copy.start()
    return copies


def wait_all(copies):
    for copy in copies:
        copy.wait()


def sub_rows(rows, width):
    pieces = [rows[:, q * width : (q + 1) * width].astype(F32) for q in range(PARTS)]
    return jnp.concatenate(pieces, axis=0).astype(BF16)


def pick_kernel(plan_hbm, length_hbm, finished_hbm, tokens_hbm, out, *scratch):
    plan, length, finished, tokens, send, sems = scratch
    pairs = [
        (plan_hbm, plan),
        (length_hbm, length),
        (finished_hbm, finished),
        (tokens_hbm, tokens),
    ]
    wait_all(start_all([pltpu.make_async_copy(*pair, sems.at[n]) for n, pair in enumerate(pairs)]))
    count = tokens.shape[0]
    shape = (send.shape[0], PARTS * count)
    row, col = iota(shape, 0), iota(shape, 1)
    source = col & (count - 1)
    wanted = by_index(row >> 3, send.shape[0] // 8, lambda d: plan[d])
    alive = by_index(source, count, alive_of(length, finished))
    chosen = (wanted == source) & ((row & 7) == (col >> 3)) & (alive > 0)
    chosen = jnp.where(chosen, 1.0, 0.0).astype(BF16)
    flat = sub_rows(tokens[...], send.shape[1])
    send[...] = jnp.dot(chosen, flat, preferred_element_type=F32).astype(BF16)
    wait_all(start_all([pltpu.make_async_copy(send, out, sems.at[0])]))


def routing_kernel(plan_hbm, length_hbm, finished_hbm, routes_hbm, score_hbm, tokens_hbm, *rest):
    scatter, gather, flat, plan, length, finished, routes, score, tokens, sems = rest
    pairs = [
        (plan_hbm, plan),
        (length_hbm, length),
        (finished_hbm, finished),
        (routes_hbm, routes),
        (score_hbm, score),
        (tokens_hbm, tokens),
    ]
    wait_all(start_all([pltpu.make_async_copy(*pair, sems.at[n]) for n, pair in enumerate(pairs)]))
    flat[...] = sub_rows(tokens[...], flat.shape[1])
    top, slots = routes.shape
    lanes = scatter.shape[0]
    experts = lanes // 8
    count = slots // 2
    names = jnp.transpose(routes[...].astype(F32))
    scores = jnp.transpose(score[...])
    expert = iota((slots, experts), 1).astype(F32)
    named = jnp.zeros((slots, experts), F32)
    weight = jnp.zeros((slots, experts), F32)
    for k in range(top):
        hit = names[:, k : k + 1] == expert
        named = jnp.where(hit, 1.0, named)
        weight = jnp.where(hit, scores[:, k : k + 1], weight)
    weight = 2.5 * weight / jnp.sum(scores, axis=1, keepdims=True)
    lower = jnp.where(iota((slots, slots), 1) < iota((slots, slots), 0), 1.0, 0.0).astype(BF16)
    position = jnp.dot(lower, named.astype(BF16), preferred_element_type=F32)
    high = weight.astype(BF16).astype(F32)
    low = weight - high
    stacked = jnp.concatenate([named, position, high, low], axis=0).astype(BF16)
    widen = iota((experts, lanes), 0) == (iota((experts, lanes), 1) >> 3)
    wide = jnp.dot(stacked, jnp.where(widen, 1.0, 0.0).astype(BF16), preferred_element_type=F32)
    lane = iota((slots, lanes), 1)
    part = lane & (PARTS - 1)
    place = ((lane >> 2) & 1).astype(F32)
    taken = (wide[:slots] > 0.5) & (wide[slots : 2 * slots] == place)
    taken = jnp.where(taken, 1.0, 0.0)

    row = iota((count, lanes), 0)
    alive = by_index(row, count, alive_of(length, finished))
    moved = jnp.zeros((count, lanes), jnp.int32)
    for d in range(count):
        moved = jnp.where(row == plan[d], 1, moved)
    stays = (alive > 0) & (moved == 0)
    half = part[:count]
    pieces = [jnp.where(stays & (half == q), taken[:count], 0.0) for q in range(PARTS)]
    for i in range(count):
        pieces.append(jnp.where(half == row, taken[count + i : count + i + 1], 0.0))
    used = len(pieces) * count
    pieces.append(jnp.zeros((scatter.shape[1] - used, lanes), F32))
    scatter[...] = jnp.transpose(jnp.concatenate(pieces, axis=0)).astype(BF16)

    pieces = []
    for start in (2 * slots, 3 * slots):
        wanted = wide[start : start + slots] * taken
        pieces += [jnp.where(part == q, wanted, 0.0) for q in range(PARTS)]
    gather[...] = jnp.concatenate(pieces, axis=0).astype(BF16)


def dispatch_kernel(scatter, tokens, arrived, out, block, sems):
    lanes, width = out.shape
    pad = scatter.shape[1] - tokens.shape[0] - arrived.shape[0]
    flat = jnp.concatenate([tokens[...], arrived[...], jnp.zeros((pad, width), BF16)], axis=0)
    copies = []
    for b in range(lanes // 256):
        part = pl.ds(b * 256, 256)
        rows = jnp.dot(scatter[part, :], flat, preferred_element_type=F32)
        block[part, :] = rows.astype(BF16)
        copies += start_all([pltpu.make_async_copy(block.at[part], out.at[part], sems.at[b])])
    wait_all(copies)


def one_hot(hit):
    return jnp.where(hit, 1.0, 0.0).astype(BF16)


def expert_kernel(recv, w_gate, w_up, w_down, out, *scratch):
    gates, ups, downs, rows, results, sent, sems = scratch
    lanes, width = recv.shape
    blocks = lanes // 256
    total = lanes // PARTS
    gate_copies, up_copies, down_copies = [], [], []
    for q in range(PARTS):
        part = pl.ds(q * width, width)
        gate_copies.append(pltpu.make_async_copy(w_gate.at[0, part, :], gates.at[q], sems.at[0, q]))
        up_copies.append(pltpu.make_async_copy(w_up.at[0, part, :], ups.at[q], sems.at[1, q]))
        down_copies.append(
            pltpu.make_async_copy(w_down.at[0, :, part], downs.at[q], sems.at[2, q])
        )
        start_all([gate_copies[q], up_copies[q]])
    start_all(down_copies)

    one, two = iota((256, 256), 0), iota((256, 256), 1)
    apart = one_hot(((one & 63) * PARTS + (one >> 6)) == two)
    together = one_hot(((two & 63) * PARTS + (two >> 6)) == one)
    used = jnp.zeros((8, total), F32)
    for b in range(blocks):
        part = recv[b * 256 : (b + 1) * 256, :]
        nonzero = jnp.where(part.astype(F32) != 0, 1.0, 0.0).astype(BF16)
        found = lax.dot_general(
            jnp.ones((8, width), BF16),
            nonzero,
            (((1,), (1,)), ((), ())),
            preferred_element_type=F32,
        )
        found = jnp.where(found > 0, 1.0, 0.0).astype(BF16)
        pool = one_hot((iota((256, total), 0) >> 2) + b * 64 == iota((256, total), 1))
        used = used + jnp.dot(found, pool, preferred_element_type=F32)
        got = jnp.dot(apart, part, preferred_element_type=F32).astype(BF16)
        for q in range(PARTS):
            rows[q, b * 64 : (b + 1) * 64, :] = got[q * 64 : (q + 1) * 64, :]
    used = jnp.where(used > 0, 1.0, 0.0)
    before = one_hot(iota((total, total), 0) < iota((total, total), 1))
    place = jnp.dot(used.astype(BF16), before, preferred_element_type=F32)
    count = jnp.sum(used[:1, :]).astype(jnp.int32)

    def body(size):
        pick = (iota((size, total), 0).astype(F32) == place[:1, :]) & (used[:1, :] > 0)
        pick = jnp.where(pick, 1.0, 0.0)
        spread = jnp.transpose(pick).astype(BF16)
        pick = pick.astype(BF16)
        packed = [
            jnp.dot(pick, rows[q], preferred_element_type=F32).astype(BF16) for q in range(PARTS)
        ]
        gate = up = None
        for q in range(PARTS):
            gate_copies[q].wait()
            more = jnp.dot(packed[q], gates[q], preferred_element_type=F32)
            gate = more if gate is None else gate + more
            up_copies[q].wait()
            more = jnp.dot(packed[q], ups[q], preferred_element_type=F32)
            up = more if up is None else up + more
        hidden = (gate / (1.0 + jnp.exp(-gate)) * up).astype(BF16)
        for q in range(PARTS):
            down_copies[q].wait()
            result = jnp.dot(hidden, downs[q], preferred_element_type=F32).astype(BF16)
            result = jnp.dot(spread, result, preferred_element_type=F32).astype(BF16)
            for b in range(blocks):
                results[b, q * 64 : (q + 1) * 64, :] = result[b * 64 : (b + 1) * 64, :]

    small = 160

    @pl.when(count <= small)
    def _():
        body(small)

    @pl.when(count > small)
    def _():
        body(total)

    copies = []
    for b in range(blocks):
        part = pl.ds(b * 256, 256)
        value = jnp.dot(together, results[b], preferred_element_type=F32).astype(BF16)
        sent[part, :] = value
        copies += start_all([pltpu.make_async_copy(sent.at[part], out.at[part], sems.at[0, b])])
    wait_all(copies)


def leave_kernel(plan, attended, own, beside):
    for n in range(own.shape[0]):
        for core, out in enumerate((own, beside)):
            row = plan[my_replica() ^ (2 * n + core)]
            kept = jnp.where(row >= 0, 1.0, 0.0)
            out[n] = (attended[jnp.maximum(row, 0)].astype(F32) * kept).astype(BF16)


def pair_kernel(own, handed, *outs):
    for n, out in enumerate(outs, 1):
        out[0] = own[n]
        out[1] = handed[n]


def land_kernel(plan, attended, handed, *rest):
    arrived, out = rest[:-1], rest[-1]
    count = attended.shape[0]
    me = my_replica()
    for s in range(count):
        moved = jnp.int32(0)
        for d in range(count):
            moved = jnp.where(plan[d] == s, 1, moved)
        kept = jnp.where(moved == 0, 1.0, 0.0)
        out[s] = (attended[s].astype(F32) * kept).astype(BF16)
    out[count + me] = jnp.zeros(out.shape[1:], BF16)
    out[count + (me ^ 1)] = handed[0]
    for n, rows in enumerate(arrived, 1):
        for core in range(2):
            out[count + (me ^ (2 * n + core))] = rows[core]


def combine_kernel(gather, recv, out):
    slots = out.shape[0]
    width = recv.shape[1]
    summed = jnp.dot(gather[...], recv[...], preferred_element_type=F32)
    half = summed.shape[0] // 2
    summed = summed[:half] + summed[half:]
    for q in range(PARTS):
        out[:, q * width : (q + 1) * width] = summed[q * slots : (q + 1) * slots].astype(BF16)


def call(kernel, outs, in_specs, cost, scratch=(), limit=32, in_hbm=False):
    shape_of = pltpu.HBM if in_hbm else jax.ShapeDtypeStruct
    shapes = [shape_of(shape, BF16) for shape in outs]
    specs = [HBM if in_hbm else VMEM] * len(outs)
    return pl.pallas_call(
        kernel,
        out_shape=shapes if len(shapes) > 1 else shapes[0],
        in_specs=in_specs,
        out_specs=specs if len(specs) > 1 else specs[0],
        scratch_shapes=list(scratch),
        compiler_params=pltpu.CompilerParams(vmem_limit_bytes=limit * 2**20),
        cost_estimate=pl.CostEstimate(flops=cost[0], bytes_accessed=cost[1], transcendentals=0),
    )


def on_device(
    tokens,
    queries,
    latent_cache,
    new_latent,
    lengths,
    finished,
    migrate,
    routes,
    route_score,
    w_gate,
    w_up,
    w_down,
):
    count, model = tokens.shape
    slots = routes.shape[0]
    replicas = lax.axis_size("replica")
    devices = replicas * lax.axis_size("expert")
    width = model // PARTS
    lanes = devices * CAP * PARTS
    hidden = w_gate.shape[2]
    plan = migrate.reshape(replicas)

    def exchange(values):
        values = values.reshape(devices, 8, width)
        values = lax.all_to_all(values, BOTH, split_axis=0, concat_axis=0, tiled=True)
        return values.reshape(lanes, width)

    def in_hbm(*values):
        return [pltpu.with_memory_space_constraint(value, pltpu.HBM) for value in values]

    integers = [
        pltpu.SMEM((replicas,), jnp.int32),
        pltpu.SMEM((count,), jnp.int32),
        pltpu.SMEM((count,), jnp.int32),
    ]
    send = call(
        pick_kernel,
        [(replicas * 8, width)],
        [HBM] * 4,
        (10**6, 10**5),
        integers
        + [
            pltpu.VMEM((count, model), BF16),
            pltpu.VMEM((replicas * 8, width), BF16),
            pltpu.SemaphoreType.DMA((4,)),
        ],
        in_hbm=True,
    )(*in_hbm(plan, lengths, finished, tokens))
    arrived = lax.all_to_all(
        send.reshape(replicas, 8, width), "replica", split_axis=0, concat_axis=0, tiled=True
    ).reshape(replicas * 8, width)
    scatter, gather, flat = call(
        routing_kernel,
        [(lanes, 128), (2 * PARTS * slots, lanes), (PARTS * count, width)],
        [HBM] * 6,
        (10**7, 10**6),
        integers
        + [
            pltpu.VMEM((routes.shape[1], slots), jnp.int32),
            pltpu.VMEM((routes.shape[1], slots), F32),
            pltpu.VMEM((count, model), BF16),
            pltpu.SemaphoreType.DMA((6,)),
        ],
    )(*in_hbm(plan, lengths, finished, routes.T, route_score.T, tokens))
    outgoing = call(
        dispatch_kernel,
        [(lanes, width)],
        [VMEM] * 3,
        (2 * 10**8, 2 * 10**6),
        [pltpu.VMEM((lanes, width), BF16), pltpu.SemaphoreType.DMA((lanes // 256,))],
        in_hbm=True,
    )(scatter, flat, arrived)
    own_length = jnp.where(finished == 0, lengths, 0)
    held = lax.optimization_barrier((queries, new_latent, outgoing))
    queries, new_latent, outgoing = held
    incoming = exchange(outgoing)

    attended = attend(queries, latent_cache, new_latent, own_length)
    def swap(values, k):
        return lax.ppermute(values, "replica", [(i, i ^ k) for i in range(replicas)])

    chips = replicas // 2
    own, beside = call(
        leave_kernel,
        [(chips, HEADS, VDIM)] * 2,
        [SMEM, VMEM],
        (10**6, 10**6),
    )(plan, attended)
    handed = swap(beside, 1)
    pairs = call(
        pair_kernel,
        [(2, HEADS, VDIM)] * (chips - 1),
        [VMEM] * 2,
        (10**6, 10**6),
    )(own, handed)
    landed = [swap(pair, 2 * n) for n, pair in enumerate(pairs, 1)]
    results = call(
        expert_kernel,
        [(lanes, width)],
        [VMEM] + [HBM] * 3,
        (10**5, 10**5),
        [
            pltpu.VMEM((PARTS, width, hidden), BF16),
            pltpu.VMEM((PARTS, width, hidden), BF16),
            pltpu.VMEM((PARTS, hidden, width), BF16),
            pltpu.VMEM((PARTS, devices * CAP, width), BF16),
            pltpu.VMEM((lanes // 256, 256, width), BF16),
            pltpu.VMEM((lanes, width), BF16),
            pltpu.SemaphoreType.DMA((3, 4)),
        ],
        46,
        True,
    )(incoming, *in_hbm(w_gate, w_up, w_down))
    *landed, results = lax.optimization_barrier((*landed, results))
    returned = exchange(results)
    attended_out = call(
        land_kernel,
        [(slots, HEADS, VDIM)],
        [SMEM] + [VMEM] * (1 + chips),
        (10**6, 4 * 10**6),
    )(plan, attended, handed, *landed).reshape(slots, HEADS * VDIM)
    expert_out = call(combine_kernel, [(slots, model)], [VMEM] * 2, (2 * 10**8, 2 * 10**6))(
        gather, returned
    )
    return (attended_out, expert_out)


def solution(mesh):
    rows = P(BOTH, None)
    blocks = P(BOTH, None, None)
    flat = P(BOTH)
    return jax.shard_map(
        on_device,
        mesh=mesh,
        in_specs=(rows, rows, blocks, rows, flat, flat, blocks, rows, rows, blocks, blocks, blocks),
        out_specs=(rows, rows),
        check_vma=False,
    )
```

```python
import jax
import jax.numpy as jnp
from jax import lax
from jax.experimental import pallas as pl
from jax.experimental.pallas import tpu as pltpu
from jax.sharding import PartitionSpec as P

HEADS = 64
VDIM = 512
LAT = 576
BOTH = ("replica", "expert")
F32 = jnp.float32
BF16 = jnp.bfloat16

PARTS = 4
CAP = 2

score_scale = 192.0 ** (-0.5)

VMEM = pl.BlockSpec(memory_space=pltpu.VMEM)
SMEM = pl.BlockSpec(memory_space=pltpu.SMEM)
HBM = pl.BlockSpec(memory_space=pltpu.HBM)


def iota(shape, dim):
    return lax.broadcasted_iota(jnp.int32, shape, dim)


def attend(query_rows, latent_rows, own_latent, live_length):
    row_count = query_rows.shape[0]
    per_head = query_rows.reshape(row_count, HEADS, LAT)
    scores = (
        jnp.einsum("nhl,ntl->nht", per_head, latent_rows, preferred_element_type=F32) * score_scale
    )
    own_score = jnp.einsum("nhl,nl->nh", per_head, own_latent, preferred_element_type=F32)
    own_score = own_score * score_scale
    visible = iota((1, 1, latent_rows.shape[1]), 2) < live_length[:, None, None]
    scores = jnp.where(visible, scores, -jnp.inf)
    largest = jnp.maximum(jnp.max(scores, axis=2), own_score)
    weights = jnp.exp(scores - largest[:, :, None])
    own_weight = jnp.exp(own_score - largest)
    denominator = jnp.sum(weights, axis=2) + own_weight
    context = jnp.einsum(
        "nht,ntv->nhv",
        weights.astype(BF16),
        latent_rows[:, :, :VDIM],
        preferred_element_type=F32,
    )
    own_rounded = lax.optimization_barrier(own_weight.astype(BF16)).astype(F32)
    context = context + own_rounded[:, :, None] * own_latent[:, None, :VDIM].astype(F32)
    normalized = context / denominator[:, :, None] * (live_length > 0).astype(F32)[:, None, None]
    return normalized.astype(BF16)


def by_index(index, count, value_of):
    spread = jnp.zeros(index.shape, jnp.int32)
    for i in range(count):
        spread = jnp.where(index == i, value_of(i), spread)
    return spread


def alive_of(length, finished):
    return lambda s: jnp.where(finished[s] == 0, length[s], 0)


def my_replica():
    return lax.axis_index("replica")


def start_all(copies):
    for copy in copies:
        copy.start()
    return copies


def wait_all(copies):
    for copy in copies:
        copy.wait()


def sub_rows(rows, width):
    pieces = [rows[:, q * width : (q + 1) * width].astype(F32) for q in range(PARTS)]
    return jnp.concatenate(pieces, axis=0).astype(BF16)


def pick_kernel(plan_hbm, length_hbm, finished_hbm, tokens_hbm, own, beside, *scratch):
    plan, length, finished, tokens, sems = scratch
    pairs = [
        (plan_hbm, plan),
        (length_hbm, length),
        (finished_hbm, finished),
        (tokens_hbm, tokens),
    ]
    wait_all(start_all([pltpu.make_async_copy(*pair, sems.at[n]) for n, pair in enumerate(pairs)]))
    count = tokens.shape[0]
    height, width = own.shape
    shape = (2 * height, PARTS * count)
    row, col = iota(shape, 0), iota(shape, 1)
    source = col & (count - 1)
    place = row >> 3
    chips = height // 8
    step = (place & (chips - 1)) * 2 + jnp.where(place < chips, 0, 1)
    wanted = by_index(step ^ my_replica(), 2 * chips, lambda d: plan[d])
    alive = by_index(source, count, alive_of(length, finished))
    chosen = (wanted == source) & ((row & 7) == (col >> 3)) & (alive > 0)
    chosen = jnp.where(chosen, 1.0, 0.0).astype(BF16)
    flat = sub_rows(tokens[...], width)
    picked = jnp.dot(chosen, flat, preferred_element_type=F32).astype(BF16)
    own[...] = picked[:height]
    beside[...] = picked[height:]


def pair_tokens_kernel(own, handed, *outs):
    mine, other = own[...].astype(F32), handed[...].astype(F32)
    for n, out in enumerate(outs, 1):
        part = slice(8 * n, 8 * n + 8)
        out[...] = jnp.concatenate([mine[part], other[part]], axis=0).astype(BF16)


def routing_kernel(plan_hbm, length_hbm, finished_hbm, routes_hbm, score_hbm, tokens_hbm, *rest):
    scatter, gather, flat, plan, length, finished, routes, score, tokens, sems = rest
    pairs = [
        (plan_hbm, plan),
        (length_hbm, length),
        (finished_hbm, finished),
        (routes_hbm, routes),
        (score_hbm, score),
        (tokens_hbm, tokens),
    ]
    wait_all(start_all([pltpu.make_async_copy(*pair, sems.at[n]) for n, pair in enumerate(pairs)]))
    flat[...] = sub_rows(tokens[...], flat.shape[1])
    top, slots = routes.shape
    lanes = scatter.shape[0]
    experts = lanes // 8
    count = slots // 2
    names = jnp.transpose(routes[...].astype(F32))
    scores = jnp.transpose(score[...])
    expert = iota((slots, experts), 1).astype(F32)
    named = jnp.zeros((slots, experts), F32)
    weight = jnp.zeros((slots, experts), F32)
    for k in range(top):
        hit = names[:, k : k + 1] == expert
        named = jnp.where(hit, 1.0, named)
        weight = jnp.where(hit, scores[:, k : k + 1], weight)
    weight = 2.5 * weight / jnp.sum(scores, axis=1, keepdims=True)
    lower = jnp.where(iota((slots, slots), 1) < iota((slots, slots), 0), 1.0, 0.0).astype(BF16)
    position = jnp.dot(lower, named.astype(BF16), preferred_element_type=F32)
    high = weight.astype(BF16).astype(F32)
    low = weight - high
    stacked = jnp.concatenate([named, position, high, low], axis=0).astype(BF16)
    widen = iota((experts, lanes), 0) == (iota((experts, lanes), 1) >> 3)
    wide = jnp.dot(stacked, jnp.where(widen, 1.0, 0.0).astype(BF16), preferred_element_type=F32)
    lane = iota((slots, lanes), 1)
    part = lane & (PARTS - 1)
    place = ((lane >> 2) & 1).astype(F32)
    taken = (wide[:slots] > 0.5) & (wide[slots : 2 * slots] == place)
    taken = jnp.where(taken, 1.0, 0.0)

    row = iota((count, lanes), 0)
    alive = by_index(row, count, alive_of(length, finished))
    moved = jnp.zeros((count, lanes), jnp.int32)
    for d in range(count):
        moved = jnp.where(row == plan[d], 1, moved)
    stays = (alive > 0) & (moved == 0)
    half = part[:count]
    pieces = [jnp.where(stays & (half == q), taken[:count], 0.0) for q in range(PARTS)]
    swapped = iota((count, count), 1) == (iota((count, count), 0) ^ my_replica())
    swapped = jnp.where(swapped, 1.0, 0.0).astype(BF16)
    landed = jnp.dot(swapped, taken[count:].astype(BF16), preferred_element_type=F32)
    for k in range(1, count):
        pieces.append(jnp.where(half == row, landed[k : k + 1], 0.0))
    used = len(pieces) * count
    pieces.append(jnp.zeros((scatter.shape[1] - used, lanes), F32))
    scatter[...] = jnp.transpose(jnp.concatenate(pieces, axis=0)).astype(BF16)

    pieces = []
    for start in (2 * slots, 3 * slots):
        wanted = wide[start : start + slots] * taken
        pieces += [jnp.where(part == q, wanted, 0.0) for q in range(PARTS)]
    gather[...] = jnp.concatenate(pieces, axis=0).astype(BF16)


def dispatch_kernel(scatter, tokens, handed, *rest):
    arrived, (out, block, sems) = rest[:-3], rest[-3:]
    lanes, width = out.shape
    pieces = [tokens[...].astype(F32), handed[...].astype(F32)[:8]]
    pieces += [rows[...].astype(F32) for rows in arrived]
    pad = scatter.shape[1] - sum(piece.shape[0] for piece in pieces)
    pieces.append(jnp.zeros((pad, width), F32))
    flat = jnp.concatenate(pieces, axis=0).astype(BF16)
    copies = []
    for b in range(lanes // 256):
        part = pl.ds(b * 256, 256)
        rows = jnp.dot(scatter[part, :], flat, preferred_element_type=F32)
        block[part, :] = rows.astype(BF16)
        copies += start_all([pltpu.make_async_copy(block.at[part], out.at[part], sems.at[b])])
    wait_all(copies)


def one_hot(hit):
    return jnp.where(hit, 1.0, 0.0).astype(BF16)


def expert_kernel(recv, w_gate, w_up, w_down, out, *scratch):
    gates, ups, downs, rows, results, sent, sems = scratch
    lanes, width = recv.shape
    blocks = lanes // 256
    total = lanes // PARTS
    gate_copies, up_copies, down_copies = [], [], []
    for q in range(PARTS):
        part = pl.ds(q * width, width)
        gate_copies.append(pltpu.make_async_copy(w_gate.at[0, part, :], gates.at[q], sems.at[0, q]))
        up_copies.append(pltpu.make_async_copy(w_up.at[0, part, :], ups.at[q], sems.at[1, q]))
        down_copies.append(
            pltpu.make_async_copy(w_down.at[0, :, part], downs.at[q], sems.at[2, q])
        )
        start_all([gate_copies[q], up_copies[q]])
    start_all(down_copies)

    one, two = iota((256, 256), 0), iota((256, 256), 1)
    apart = one_hot(((one & 63) * PARTS + (one >> 6)) == two)
    together = one_hot(((two & 63) * PARTS + (two >> 6)) == one)
    used = jnp.zeros((8, total), F32)
    for b in range(blocks):
        part = recv[b * 256 : (b + 1) * 256, :]
        nonzero = jnp.where(part.astype(F32) != 0, 1.0, 0.0).astype(BF16)
        found = lax.dot_general(
            jnp.ones((8, width), BF16),
            nonzero,
            (((1,), (1,)), ((), ())),
            preferred_element_type=F32,
        )
        found = jnp.where(found > 0, 1.0, 0.0).astype(BF16)
        pool = one_hot((iota((256, total), 0) >> 2) + b * 64 == iota((256, total), 1))
        used = used + jnp.dot(found, pool, preferred_element_type=F32)
        got = jnp.dot(apart, part, preferred_element_type=F32).astype(BF16)
        for q in range(PARTS):
            rows[q, b * 64 : (b + 1) * 64, :] = got[q * 64 : (q + 1) * 64, :]
    used = jnp.where(used > 0, 1.0, 0.0)
    before = one_hot(iota((total, total), 0) < iota((total, total), 1))
    place = jnp.dot(used.astype(BF16), before, preferred_element_type=F32)
    count = jnp.sum(used[:1, :]).astype(jnp.int32)

    def body(size):
        pick = (iota((size, total), 0).astype(F32) == place[:1, :]) & (used[:1, :] > 0)
        pick = jnp.where(pick, 1.0, 0.0)
        spread = jnp.transpose(pick).astype(BF16)
        pick = pick.astype(BF16)
        packed = [
            jnp.dot(pick, rows[q], preferred_element_type=F32).astype(BF16) for q in range(PARTS)
        ]
        gate = up = None
        for q in range(PARTS):
            gate_copies[q].wait()
            more = jnp.dot(packed[q], gates[q], preferred_element_type=F32)
            gate = more if gate is None else gate + more
            up_copies[q].wait()
            more = jnp.dot(packed[q], ups[q], preferred_element_type=F32)
            up = more if up is None else up + more
        hidden = (gate / (1.0 + jnp.exp(-gate)) * up).astype(BF16)
        for q in range(PARTS):
            down_copies[q].wait()
            result = jnp.dot(hidden, downs[q], preferred_element_type=F32).astype(BF16)
            result = jnp.dot(spread, result, preferred_element_type=F32).astype(BF16)
            for b in range(blocks):
                results[b, q * 64 : (q + 1) * 64, :] = result[b * 64 : (b + 1) * 64, :]

    small = 160

    @pl.when(count <= small)
    def _():
        body(small)

    @pl.when(count > small)
    def _():
        body(total)

    copies = []
    for b in range(blocks):
        part = pl.ds(b * 256, 256)
        value = jnp.dot(together, results[b], preferred_element_type=F32).astype(BF16)
        sent[part, :] = value
        copies += start_all([pltpu.make_async_copy(sent.at[part], out.at[part], sems.at[0, b])])
    wait_all(copies)


def leave_kernel(plan, attended, own, beside):
    for n in range(own.shape[0]):
        for core, out in enumerate((own, beside)):
            row = plan[my_replica() ^ (2 * n + core)]
            kept = jnp.where(row >= 0, 1.0, 0.0)
            out[n] = (attended[jnp.maximum(row, 0)].astype(F32) * kept).astype(BF16)


def pair_kernel(own, handed, *outs):
    for n, out in enumerate(outs, 1):
        out[0] = own[n]
        out[1] = handed[n]


def land_kernel(plan, attended, handed, *rest):
    arrived, out = rest[:-1], rest[-1]
    count = attended.shape[0]
    me = my_replica()
    for s in range(count):
        moved = jnp.int32(0)
        for d in range(count):
            moved = jnp.where(plan[d] == s, 1, moved)
        kept = jnp.where(moved == 0, 1.0, 0.0)
        out[s] = (attended[s].astype(F32) * kept).astype(BF16)
    out[count + me] = jnp.zeros(out.shape[1:], BF16)
    out[count + (me ^ 1)] = handed[0]
    for n, rows in enumerate(arrived, 1):
        for core in range(2):
            out[count + (me ^ (2 * n + core))] = rows[core]


def combine_kernel(gather, recv, out):
    slots = out.shape[0]
    width = recv.shape[1]
    summed = jnp.dot(gather[...], recv[...], preferred_element_type=F32)
    half = summed.shape[0] // 2
    summed = summed[:half] + summed[half:]
    for q in range(PARTS):
        out[:, q * width : (q + 1) * width] = summed[q * slots : (q + 1) * slots].astype(BF16)


def call(kernel, outs, in_specs, cost, scratch=(), limit=32, in_hbm=False):
    shape_of = pltpu.HBM if in_hbm else jax.ShapeDtypeStruct
    shapes = [shape_of(shape, BF16) for shape in outs]
    specs = [HBM if in_hbm else VMEM] * len(outs)
    return pl.pallas_call(
        kernel,
        out_shape=shapes if len(shapes) > 1 else shapes[0],
        in_specs=in_specs,
        out_specs=specs if len(specs) > 1 else specs[0],
        scratch_shapes=list(scratch),
        compiler_params=pltpu.CompilerParams(vmem_limit_bytes=limit * 2**20),
        cost_estimate=pl.CostEstimate(flops=cost[0], bytes_accessed=cost[1], transcendentals=0),
    )


def on_device(
    tokens,
    queries,
    latent_cache,
    new_latent,
    lengths,
    finished,
    migrate,
    routes,
    route_score,
    w_gate,
    w_up,
    w_down,
):
    count, model = tokens.shape
    slots = routes.shape[0]
    replicas = lax.axis_size("replica")
    devices = replicas * lax.axis_size("expert")
    width = model // PARTS
    lanes = devices * CAP * PARTS
    hidden = w_gate.shape[2]
    plan = migrate.reshape(replicas)

    def exchange(values):
        values = values.reshape(devices, 8, width)
        values = lax.all_to_all(values, BOTH, split_axis=0, concat_axis=0, tiled=True)
        return values.reshape(lanes, width)

    def in_hbm(*values):
        return [pltpu.with_memory_space_constraint(value, pltpu.HBM) for value in values]

    integers = [
        pltpu.SMEM((replicas,), jnp.int32),
        pltpu.SMEM((count,), jnp.int32),
        pltpu.SMEM((count,), jnp.int32),
    ]
    def swap(values, k):
        return lax.ppermute(values, "replica", [(i, i ^ k) for i in range(replicas)])

    chips = replicas // 2
    tokens_own, tokens_beside = call(
        pick_kernel,
        [(chips * 8, width)] * 2,
        [HBM] * 4,
        (10**6, 10**5),
        integers
        + [
            pltpu.VMEM((count, model), BF16),
            pltpu.SemaphoreType.DMA((4,)),
        ],
    )(*in_hbm(plan, lengths, finished, tokens))
    tokens_handed = swap(tokens_beside, 1)
    tokens_paired = call(
        pair_tokens_kernel,
        [(16, width)] * (chips - 1),
        [VMEM] * 2,
        (10**5, 10**5),
    )(tokens_own, tokens_handed)
    arrived = [swap(pair, 2 * n) for n, pair in enumerate(tokens_paired, 1)]
    scatter, gather, flat = call(
        routing_kernel,
        [(lanes, 128), (2 * PARTS * slots, lanes), (PARTS * count, width)],
        [HBM] * 6,
        (10**7, 10**6),
        integers
        + [
            pltpu.VMEM((routes.shape[1], slots), jnp.int32),
            pltpu.VMEM((routes.shape[1], slots), F32),
            pltpu.VMEM((count, model), BF16),
            pltpu.SemaphoreType.DMA((6,)),
        ],
    )(*in_hbm(plan, lengths, finished, routes.T, route_score.T, tokens))
    outgoing = call(
        dispatch_kernel,
        [(lanes, width)],
        [VMEM] * (2 + chips),
        (2 * 10**8, 2 * 10**6),
        [pltpu.VMEM((lanes, width), BF16), pltpu.SemaphoreType.DMA((lanes // 256,))],
        in_hbm=True,
    )(scatter, flat, tokens_handed, *arrived)
    own_length = jnp.where(finished == 0, lengths, 0)
    held = lax.optimization_barrier((queries, new_latent, outgoing))
    queries, new_latent, outgoing = held
    incoming = exchange(outgoing)

    attended = attend(queries, latent_cache, new_latent, own_length)
    own, beside = call(
        leave_kernel,
        [(chips, HEADS, VDIM)] * 2,
        [SMEM, VMEM],
        (10**6, 10**6),
    )(plan, attended)
    handed = swap(beside, 1)
    pairs = call(
        pair_kernel,
        [(2, HEADS, VDIM)] * (chips - 1),
        [VMEM] * 2,
        (10**6, 10**6),
    )(own, handed)
    landed = [swap(pair, 2 * n) for n, pair in enumerate(pairs, 1)]
    results = call(
        expert_kernel,
        [(lanes, width)],
        [VMEM] + [HBM] * 3,
        (10**5, 10**5),
        [
            pltpu.VMEM((PARTS, width, hidden), BF16),
            pltpu.VMEM((PARTS, width, hidden), BF16),
            pltpu.VMEM((PARTS, hidden, width), BF16),
            pltpu.VMEM((PARTS, devices * CAP, width), BF16),
            pltpu.VMEM((lanes // 256, 256, width), BF16),
            pltpu.VMEM((lanes, width), BF16),
            pltpu.SemaphoreType.DMA((3, 4)),
        ],
        46,
        True,
    )(incoming, *in_hbm(w_gate, w_up, w_down))
    *landed, results = lax.optimization_barrier((*landed, results))
    returned = exchange(results)
    attended_out = call(
        land_kernel,
        [(slots, HEADS, VDIM)],
        [SMEM] + [VMEM] * (1 + chips),
        (10**6, 4 * 10**6),
    )(plan, attended, handed, *landed).reshape(slots, HEADS * VDIM)
    expert_out = call(combine_kernel, [(slots, model)], [VMEM] * 2, (2 * 10**8, 2 * 10**6))(
        gather, returned
    )
    return (attended_out, expert_out)


def solution(mesh):
    rows = P(BOTH, None)
    blocks = P(BOTH, None, None)
    flat = P(BOTH)
    return jax.shard_map(
        on_device,
        mesh=mesh,
        in_specs=(rows, rows, blocks, rows, flat, flat, blocks, rows, rows, blocks, blocks, blocks),
        out_specs=(rows, rows),
        check_vma=False,
    )
```
